256 devices in a mesh: tm: 32 (over z, y), space: 8 (over x, core).
Axes of the slice: x: 4, y: 4, z: 8, core: 2. Of those that a mesh axis runs over, the one named last changes fastest.
Arguments:
- c_values: float32 [32, 2, 512, 512], P('tm', None, 'space'), may hold values from -2.5 to 2.5
- viscosity: float32 [512, 512], P('space'), may hold values from 0.05 to 0.2
Outputs:
- corrected: float32 [32, 2, 512, 512], P('tm', None, 'space')
- advanced: float32 [32, 2, 512, 512], P('tm', None, 'space')
- defect: float32 [32, 2, 512, 512], P('tm', None, 'space')
The draws below stay inside these ranges and needn't reach their ends.
All inputs are finite; a program needn't handle non-finite values.
Results may differ from the reference program's by a relative error of at most 0.00002.
Values sent between devices are 32-bit elements; how exact they have to be, the bound alone decides.
No kernel may reach another device: no remote copies, remote signals or barrier semaphores. Data moves between devices by JAX's collectives and lax.ppermute only.
A program may use at most 256 MiB of HBM per device.

```python
import math
import jax
import jax.numpy as jnp
from jax import lax

NY = 512
STEPS = 8
SLICES = 32
NX = 512


def levels(own_key, shape, cuts, least, top_value):
    def one(axis_at, shards_of):
        draws = jax.random.uniform(jax.random.fold_in(jax.random.fold_in(own_key, 6), axis_at), (shards_of,), jnp.float32, least / len(cuts), top_value / len(cuts))
        return jnp.repeat(jnp.exp(draws), shape[axis_at] // shards_of).reshape((-1,) + (1,) * (len(shape) - axis_at - 1))

    loudness = one(*cuts[0])
    for cut in cuts[1:]:
        loudness = loudness * one(*cut)
    return loudness


def normal_values(rng, extent, scale, most, pieces=(), dtype=jnp.bfloat16):
    result = jax.random.normal(rng, extent, jnp.float32) * scale
    if len(pieces) > 0:
        result = levels(rng, extent, pieces, -0.22, 0.18) * result
    return jnp.clip(result, min=-most, max=most).astype(dtype)


def setup_inputs(seed: int = 0) -> dict:
    splits = jax.random.split(jax.random.key(seed), 3)
    c_values = normal_values(splits[0], (SLICES, 2, NX, NY), 0.5, 2.5, ((0, 32), (2, 8)), jnp.float32)
    viscosity = jnp.clip(jnp.exp(math.log(0.2) - 1.3862944 * jax.random.uniform(splits[1], (NX, NY), jnp.float32) ** levels(splits[1], (NX, NY), ((0, 8),), -0.2, 0.2)), 0.05, 0.2)
    return {"c_values": c_values, "viscosity": viscosity}


advect_scale = 0.1
coarse_size = 1.0


def tendency(state, viscosity):
    u_part = state[..., 0, :, :]
    v_part = state[..., 1, :, :]
    face_xp = 0.5 * (viscosity + jnp.roll(viscosity, -1, -2))
    face_xm = jnp.roll(face_xp, 1, -2)
    face_yp = 0.5 * (viscosity + jnp.roll(viscosity, -1, -1))
    face_ym = jnp.roll(face_yp, 1, -1)

    def one_field(field):
        below = jnp.roll(field, -1, -2)
        above = jnp.roll(field, 1, -2)
        right_cell = jnp.roll(field, -1, -1)
        left_cell = jnp.roll(field, 1, -1)
        carried = u_part * (0.5 * (below - above)) + v_part * (0.5 * (right_cell - left_cell))
        spread = face_xp * (below - field) - face_xm * (field - above) + face_yp * (right_cell - field) - face_ym * (field - left_cell)
        return -advect_scale * carried + spread

    return jnp.stack([one_field(u_part), one_field(v_part)], axis=-3)


def heun_step(state, viscosity, size):
    first = tendency(state, viscosity)
    midpoint = state + size * first
    second = tendency(midpoint, viscosity)
    return state + 0.5 * size * (first + second)


def fine_march(state, viscosity):
    for step in range(STEPS):
        state = heun_step(state, viscosity, coarse_size / STEPS)
    return state


def reference(c_values, viscosity):
    forward = fine_march(c_values, viscosity)
    guess = heun_step(c_values, viscosity, coarse_size)
    tau = forward - guess
    defect = jnp.concatenate([jnp.zeros_like(c_values[:1]), forward[:-1] - c_values[1:]], axis=0)

    def advance(carry, term):
        nxt = heun_step(carry, viscosity, coarse_size) + term
        return nxt, nxt

    last, chain = lax.scan(advance, c_values[0], tau[:-1])
    corrected = jnp.concatenate([c_values[:1], chain], axis=0)
    advanced = fine_march(corrected, viscosity)
    return corrected, advanced, defect
```

```python
import functools

import jax
import jax.numpy as jnp
from jax import lax
from jax.experimental import pallas as pl
from jax.experimental.pallas import tpu as pltpu
from jax.sharding import PartitionSpec as P

STEPS = 8
GROUP = 8
STRIP = 8
HALO = 16
LANES = 128
WINDOW = STRIP + 2 * HALO
advect_scale = 0.1
coarse_size = 1.0
f32 = jnp.float32


def shift_up(plane):
    return pltpu.roll(plane, 1, 0)


def shift_down(plane):
    return pltpu.roll(plane, plane.shape[0] - 1, 0)


def left_of(x):
    return pltpu.roll(x, 1, 1)


def right_of(x):
    return pltpu.roll(x, x.shape[1] - 1, 1)


def make_coefs(planes, size, coef):
    cx, cyp, cym, dd = coef
    n = len(planes)
    faces = []
    for i in range(n):
        below = planes[i + 1] if i + 1 < n else shift_down(planes[0])
        faces.append((0.5 * size) * (planes[i] + below))
    first = shift_up(faces[n - 1])
    cx[0] = first
    for i in range(n):
        cx[i + 1] = faces[i]
        nyp = (0.5 * size) * (planes[i] + right_of(planes[i]))
        nym = left_of(nyp)
        cyp[i] = nyp
        cym[i] = nym
        nxm = faces[i - 1] if i > 0 else first
        dd[i] = 1.0 - ((faces[i] + nxm) + (nyp + nym))


def euler(src, coef, size, n, emit):
    cx, cyp, cym, dd = coef
    k = 0.5 * advect_scale * size
    above = [shift_up(src[c, n - 1]) for c in range(2)]
    here = [src[c, 0] for c in range(2)]
    first = here
    for i in range(n):
        if i + 1 < n:
            below = [src[c, i + 1] for c in range(2)]
        else:
            below = [shift_down(first[c]) for c in range(2)]
        ku = k * here[0]
        kv = k * here[1]
        wxp = cx[i + 1] - ku
        wxm = cx[i] + ku
        wyp = cyp[i] - kv
        wym = cym[i] + kv
        d = dd[i]
        res = []
        for c in range(2):
            f = here[c]
            res.append(
                (d * f + (wxp * below[c] + wxm * above[c]))
                + (wyp * right_of(f) + wym * left_of(f))
            )
        emit(i, res)
        above, here = here, below


def heun(src, mid, dst, coef, size, n, extra=None):
    def to_mid(i, res):
        for c in range(2):
            mid[c, i] = res[c]

    euler(src, coef, size, n, to_mid)

    def to_dst(i, res):
        for c in range(2):
            out = 0.5 * (src[c, i] + res[c])
            if extra is not None:
                out = out + extra(c, i)
            dst[c, i] = out

    euler(mid, coef, size, n, to_dst)


def plane(nat, i, n):
    return jnp.concatenate([nat[b, pl.ds(i, 8, stride=n), :] for b in range(nat.shape[0])], axis=1)


def put_plane(nat, i, n, value):
    for b in range(nat.shape[0]):
        nat[b, pl.ds(i, 8, stride=n), :] = value[:, b * LANES : (b + 1) * LANES]


def load_planes(nat, n):
    return [plane(nat, i, n) for i in range(n)]


def fill(nat, at, ref, start, count):
    for b in range(nat.shape[0]):
        nat[b, at : at + count, :] = ref[start : start + count, b * LANES : (b + 1) * LANES]


def whole(nat, start, count):
    return jnp.concatenate([nat[b, start : start + count, :] for b in range(nat.shape[0])], axis=1)


def forward_kernel(where_ref, c_ref, clo_ref, chi_ref, n_ref, nlo_ref, nhi_ref,
                   fwd_ref, tau_ref, nwin_ref,
                   nat, vnat, w, mid, tau, cf, cc):
    n = 16
    rows = c_ref.shape[1]
    edge = 2 * HALO
    for c in range(2):
        fill(nat.at[c], 0, clo_ref.at[c], rows - edge, edge)
        fill(nat.at[c], edge, c_ref.at[c], 0, rows)
        fill(nat.at[c], edge + rows, chi_ref.at[c], 0, edge)
    fill(vnat, 0, nlo_ref, rows - edge, edge)
    fill(vnat, edge, n_ref, 0, rows)
    fill(vnat, edge + rows, nhi_ref, 0, edge)
    position = where_ref[0]
    start = pl.multiple_of(lax.rem(position, GROUP) * STRIP + HALO, 8)
    nwin_ref[...] = vnat[:, pl.ds(start, WINDOW), :]

    visc = load_planes(vnat, n)
    make_coefs(visc, coarse_size, [cc.at[0], cc.at[1], cc.at[2], cc.at[3]])
    fine = coarse_size / STEPS
    make_coefs(visc, fine, [cf.at[0], cf.at[1], cf.at[2], cf.at[3]])
    coef_c = [cc.at[i] for i in range(4)]
    coef_f = [cf.at[i] for i in range(4)]
    for c in range(2):
        for i in range(n):
            w[c, i] = plane(nat.at[c], i, n)
    heun(w, mid, tau, coef_c, coarse_size, n)

    def step(_, carry):
        heun(w, mid, w, coef_f, fine, n)
        return carry

    lax.fori_loop(0, STEPS, step, 0)
    keep = jnp.where(position == 0, 0.0, 1.0).astype(f32)
    for c in range(2):
        for i in range(n):
            put_plane(nat.at[c], i, n, w[c, i])
        fwd_ref[c] = whole(nat.at[c], edge, rows)
        for i in range(n):
            put_plane(nat.at[c], i, n, w[c, i] - keep * tau[c, i])
        for p in range(GROUP):
            tau_ref[p, c] = nat[c, :, HALO + p * STRIP : HALO + p * STRIP + WINDOW, :]


def chain_kernel(stage, where_ref, tau_ref, nwin_ref, m2, m1, own, p1, p2, corr_in,
                 corr_ref, last_ref,
                 nat, w, mid, cc, part, sem):
    n = 5
    position = where_ref[0]

    @pl.when(position // GROUP == stage)
    def _():
        visc = load_planes(nwin_ref, n)
        coef = [cc.at[i] for i in range(4)]
        make_coefs(visc, coarse_size, coef)

        def keep(t):
            for c in range(2):
                for i in range(n):
                    put_plane(nat.at[c], i, n, w[c, i])
                part[t, c] = nat[c, :, HALO : HALO + STRIP, :]

        if stage == 0:
            for c in range(2):
                part[0, c] = jnp.zeros_like(part[0, c])
                for i in range(n):
                    w[c, i] = plane(tau_ref.at[0, c], i, n)
        else:
            for c in range(2):
                for k, ref in enumerate((m2, m1, own, p1, p2)):
                    nat[c, :, k * STRIP : (k + 1) * STRIP, :] = ref[c]
                part[0, c] = own[c]
                for i in range(n):
                    w[c, i] = plane(nat.at[c], i, n)
            heun(w, mid, w, coef, coarse_size, n,
                 lambda c, i: plane(tau_ref.at[0, c], i, n))
        keep(1)

        def step(t, carry):
            heun(w, mid, w, coef, coarse_size, n,
                 lambda c, i: plane(tau_ref.at[t, c], i, n))
            keep(t + 1)
            return carry

        lax.fori_loop(1, GROUP, step, 0)
        last_ref[...] = part[GROUP]
        copy = pltpu.make_async_copy(part.at[pl.ds(0, GROUP)], corr_ref, sem)
        copy.start()
        copy.wait()


def final_kernel(where_ref, got_ref, lo_ref, hi_ref, c_ref, clo_ref, chi_ref,
                 n_ref, nlo_ref, nhi_ref, handed_ref,
                 corr_ref, adv_ref, defect_ref,
                 nat, vnat, w, mid, cf):
    n = 12
    rows = c_ref.shape[1]
    position = where_ref[0]
    fill(vnat, 0, nlo_ref, rows - HALO, HALO)
    fill(vnat, HALO, n_ref, 0, rows)
    fill(vnat, HALO + rows, nhi_ref, 0, HALO)
    fine = coarse_size / STEPS
    coef = [cf.at[i] for i in range(4)]
    make_coefs(load_planes(vnat, n), fine, coef)

    @pl.when(position == 0)
    def _():
        for c in range(2):
            fill(nat.at[c], 0, clo_ref.at[c], rows - HALO, HALO)
            fill(nat.at[c], HALO, c_ref.at[c], 0, rows)
            fill(nat.at[c], HALO + rows, chi_ref.at[c], 0, HALO)
            defect_ref[0, c] = jnp.zeros_like(c_ref[c])

    @pl.when(position != 0)
    def _():
        for c in range(2):
            for k in range(2):
                nat[c, :, k * STRIP : (k + 1) * STRIP, :] = lo_ref[k, c]
                nat[c, :, HALO + rows + k * STRIP : HALO + rows + (k + 1) * STRIP, :] = hi_ref[k, c]
            for p in range(GROUP):
                nat[c, :, HALO + p * STRIP : HALO + (p + 1) * STRIP, :] = got_ref[p, c]
            defect_ref[0, c] = handed_ref[c] - c_ref[c]

    for c in range(2):
        corr_ref[0, c] = whole(nat.at[c], HALO, rows)
        for i in range(n):
            w[c, i] = plane(nat.at[c], i, n)

    def step(_, carry):
        heun(w, mid, w, coef, fine, n)
        return carry

    lax.fori_loop(0, STEPS, step, 0)
    for c in range(2):
        for i in range(n):
            put_plane(nat.at[c], i, n, w[c, i])
        adv_ref[0, c] = whole(nat.at[c], HALO, rows)


VMEM = pl.BlockSpec(memory_space=pltpu.VMEM)
SMEM = pl.BlockSpec(memory_space=pltpu.SMEM)
ANY = pl.BlockSpec(memory_space=pl.ANY)
LIMIT = 48 * 1024 * 1024


def shards(c_values, viscosity):
    c = c_values[0]
    _, rows, cols = c.shape
    ring = lax.axis_size("space")
    intervals = lax.axis_size("tm")
    up = [(i, (i + 1) % ring) for i in range(ring)]
    down = [(b, a) for a, b in up]
    where = lax.axis_index("tm").reshape(1).astype(jnp.int32)
    shape = lambda *s: jax.ShapeDtypeStruct(s, f32)
    vm = lambda *s: pltpu.VMEM(s, f32)

    clo = lax.ppermute(c, "space", up)
    chi = lax.ppermute(c, "space", down)
    nlo = lax.ppermute(viscosity, "space", up)
    nhi = lax.ppermute(viscosity, "space", down)

    blocks = cols // LANES
    n = 16
    forward, tau, nwin = pl.pallas_call(
        forward_kernel,
        out_shape=(shape(2, rows, cols), shape(GROUP, 2, blocks, WINDOW, LANES), shape(blocks, WINDOW, LANES)),
        in_specs=[SMEM] + [VMEM] * 6,
        out_specs=(VMEM, VMEM, VMEM),
        scratch_shapes=[
            vm(2, blocks, 128, LANES), vm(blocks, 128, LANES), vm(2, n, 8, cols), vm(2, n, 8, cols), vm(2, n, 8, cols),
            vm(4, n + 1, 8, cols), vm(4, n + 1, 8, cols),
        ],
        compiler_params=pltpu.CompilerParams(vmem_limit_bytes=LIMIT),
        name="forward",
    )(where, c, clo, chi, viscosity, nlo, nhi)

    groups = [[g * GROUP + j for j in range(GROUP)] for g in range(intervals // GROUP)]
    taus = lax.all_to_all(tau, "tm", 0, 0, axis_index_groups=groups)
    handed = lax.ppermute(forward, "tm", [(i, i + 1) for i in range(intervals - 1)])

    strips = ring * GROUP
    pieces = [jnp.zeros((2, blocks, STRIP, LANES), f32)] * 5
    corr = jnp.zeros((GROUP, 2, blocks, STRIP, LANES), f32)
    for stage in range(intervals // GROUP):
        n = 5
        corr, last = pl.pallas_call(
            functools.partial(chain_kernel, stage),
            out_shape=(shape(GROUP, 2, blocks, STRIP, LANES), shape(2, blocks, STRIP, LANES)),
            in_specs=[SMEM] + [VMEM] * 7 + [ANY],
            out_specs=(ANY, VMEM),
            scratch_shapes=[
                vm(2, blocks, WINDOW, LANES), vm(2, n, 8, cols), vm(2, n, 8, cols), vm(4, n + 1, 8, cols),
                vm(GROUP + 1, 2, blocks, STRIP, LANES), pltpu.SemaphoreType.DMA,
            ],
            input_output_aliases={8: 0},
            compiler_params=pltpu.CompilerParams(vmem_limit_bytes=LIMIT),
            name="chain%d" % stage,
        )(where, taus, nwin, *pieces, corr)
        if stage + 1 < intervals // GROUP:
            pieces = []
            for delta in (2, 1, 0, -1, -2):
                pairs = []
                for j in range(GROUP):
                    for s in range(ring):
                        to = (s * GROUP + j + delta) % strips
                        source = (stage * GROUP + j) * ring + s
                        target = ((stage + 1) * GROUP + to % GROUP) * ring + to // GROUP
                        pairs.append((source, target))
                pieces.append(lax.ppermute(last, ("tm", "space"), pairs))

    got = lax.all_to_all(corr, "tm", 0, 0, axis_index_groups=groups)
    lo = lax.ppermute(got[GROUP - 2 :], "space", up)
    hi = lax.ppermute(got[:2], "space", down)

    n = 12
    return pl.pallas_call(
        final_kernel,
        out_shape=(shape(1, 2, rows, cols),) * 3,
        in_specs=[SMEM] + [VMEM] * 10,
        out_specs=(VMEM,) * 3,
        scratch_shapes=[
            vm(2, blocks, 96, LANES), vm(blocks, 96, LANES), vm(2, n, 8, cols), vm(2, n, 8, cols), vm(4, n + 1, 8, cols),
        ],
        compiler_params=pltpu.CompilerParams(vmem_limit_bytes=LIMIT),
        name="final",
    )(where, got, lo, hi, c, clo, chi, viscosity, nlo, nhi, handed)


def solution(mesh):
    return jax.shard_map(
        shards,
        mesh=mesh,
        in_specs=(P("tm", None, "space", None), P("space", None)),
        out_specs=(P("tm", None, "space", None),) * 3,
        check_vma=False,
    )
```

```python
import functools

import jax
import jax.numpy as jnp
from jax import lax
from jax.experimental import pallas as pl
from jax.experimental.pallas import tpu as pltpu
from jax.sharding import PartitionSpec as P

STEPS = 8
GROUP = 8
STRIP = 16
HALO = 16
EDGE = 32
WINDOW = STRIP + 2 * HALO
LANES = 128
SPLIT = 4
advect_scale = 0.1
coarse_size = 1.0
COARSE = 0.5 * advect_scale * coarse_size
FINE = COARSE / STEPS
f32 = jnp.float32


def shift_up(plane):
    return pltpu.roll(plane, 1, 0)


def shift_down(plane):
    return pltpu.roll(plane, plane.shape[0] - 1, 0)


def left_of(x):
    return pltpu.roll(x, 1, 1)


def right_of(x):
    return pltpu.roll(x, x.shape[1] - 1, 1)


def make_coefs(planes, size, coef):
    cx, cyp, cym, dd = coef
    n = len(planes)
    faces = []
    for i in range(n):
        below = planes[i + 1] if i + 1 < n else shift_down(planes[0])
        faces.append((0.5 * size) * (planes[i] + below))
    first = shift_up(faces[n - 1])
    cx[0] = first
    for i in range(n):
        cx[i + 1] = faces[i]
        nyp = (0.5 * size) * (planes[i] + right_of(planes[i]))
        nym = left_of(nyp)
        cyp[i] = nyp
        cym[i] = nym
        nxm = faces[i - 1] if i > 0 else first
        dd[i] = 1.0 - ((faces[i] + nxm) + (nyp + nym))


def euler(src, coef, n, emit):
    cx, cyp, cym, dd = coef
    above = [shift_up(src[c, n - 1]) for c in range(2)]
    here = [src[c, 0] for c in range(2)]
    first = here
    for i in range(n):
        if i + 1 < n:
            below = [src[c, i + 1] for c in range(2)]
        else:
            below = [shift_down(first[c]) for c in range(2)]
        wxp = cx[i + 1] - here[0]
        wxm = cx[i] + here[0]
        wyp = cyp[i] - here[1]
        wym = cym[i] + here[1]
        d = dd[i]
        res = []
        for c in range(2):
            f = here[c]
            res.append(
                (d * f + (wxp * below[c] + wxm * above[c]))
                + (wyp * right_of(f) + wym * left_of(f))
            )
        emit(i, res)
        above, here = here, below


def heun(src, mid, dst, coef, n, extra=None):
    def to_mid(i, res):
        for c in range(2):
            mid[c, i] = res[c]

    euler(src, coef, n, to_mid)

    def to_dst(i, res):
        for c in range(2):
            out = 0.5 * (src[c, i] + res[c])
            if extra is not None:
                out = out + extra(c, i)
            dst[c, i] = out

    euler(mid, coef, n, to_dst)


def plane(nat, i, n):
    return jnp.concatenate([nat[b, pl.ds(i, 8, stride=n), :] for b in range(nat.shape[0])], axis=1)


def put_plane(nat, i, n, value):
    for b in range(nat.shape[0]):
        nat[b, pl.ds(i, 8, stride=n), :] = value[:, b * LANES : (b + 1) * LANES]


def load_planes(nat, n):
    return [plane(nat, i, n) for i in range(n)]


def copies(pairs, sem):
    started = [pltpu.make_async_copy(a, b, sem.at[i]) for i, (a, b) in enumerate(pairs)]
    for copy in started:
        copy.start()
    return started


def edges_kernel(c_ref, n_ref, top_ref, bottom_ref, held, sem):
    rows = n_ref.shape[0]
    pairs, later = [], []
    for k, (out, start) in enumerate(((top_ref, 0), (bottom_ref, rows - EDGE))):
        pairs.append((c_ref.at[0, :, pl.ds(start, EDGE), :], held.at[k, pl.ds(0, 2)]))
        pairs.append((n_ref.at[pl.ds(start, EDGE), :], held.at[k, 2]))
        later += [(held.at[k, pl.ds(0, 2)], out.at[pl.ds(0, 2)]), (held.at[k, 2], out.at[2])]
    started = copies(pairs, sem)
    sent = []
    for i, copy in enumerate(started):
        copy.wait()
        sent += copies([later[i]], sem.at[pl.ds(4 + i, 1)])
    for copy in sent:
        copy.wait()


def load_kernel(c_ref, n_ref, out_ref, sem):
    pairs = [(c_ref.at[0], out_ref.at[pl.ds(0, 2)]), (n_ref, out_ref.at[2])]
    for copy in copies(pairs, sem):
        copy.wait()


def cut(b):
    return pl.ds(b * LANES, LANES)


def forward_kernel(where_ref, own_ref, lo_ref, hi_ref,
                   fwd_ref, tau_ref, nwin_ref,
                   nat, fnat, w, mid, tau, cf, cc, sem):
    n = 16
    blocks = nat.shape[1]
    rows = own_ref.shape[1]
    pairs = []
    for b in range(blocks):
        mine = pl.ds(EDGE, rows)
        pairs.append((own_ref.at[2, :, cut(b)], nat.at[2, b, mine, :]))
        pairs.append((lo_ref.at[2, :, cut(b)], nat.at[2, b, pl.ds(0, EDGE), :]))
        pairs.append((hi_ref.at[2, :, cut(b)], nat.at[2, b, pl.ds(EDGE + rows, EDGE), :]))
    for b in range(blocks):
        both = pl.ds(0, 2)
        pairs.append((own_ref.at[both, :, cut(b)], nat.at[both, b, mine, :]))
        pairs.append((lo_ref.at[both, :, cut(b)], nat.at[both, b, pl.ds(0, EDGE), :]))
        pairs.append((hi_ref.at[both, :, cut(b)], nat.at[both, b, pl.ds(EDGE + rows, EDGE), :]))
    started = copies(pairs, sem)
    for copy in started[: 3 * blocks]:
        copy.wait()
    position = where_ref[0]
    vnat = nat.at[2]
    start = pl.multiple_of(lax.rem(position, SPLIT) * STRIP + HALO, 8)
    nwin_ref[...] = nat[2, :, pl.ds(start, WINDOW), :]
    visc = load_planes(vnat, n)
    coef_c = [cc.at[i] for i in range(4)]
    coef_f = [cf.at[i] for i in range(4)]
    make_coefs(visc, coarse_size, coef_c)
    make_coefs(visc, coarse_size / STEPS, coef_f)
    for copy in started[3 * blocks :]:
        copy.wait()
    for c in range(2):
        for i in range(n):
            w[c, i] = COARSE * plane(nat.at[c], i, n)
    heun(w, mid, tau, coef_c, n)
    for c in range(2):
        for i in range(n):
            w[c, i] = w[c, i] * (FINE / COARSE)

    def step(_, carry):
        heun(w, mid, w, coef_f, n)
        return carry

    lax.fori_loop(0, STEPS, step, 0)
    keep = jnp.where(position == 0, 0.0, 1.0).astype(f32)
    for c in range(2):
        for i in range(n):
            end = w[c, i] * (COARSE / FINE)
            put_plane(nat.at[c], i, n, end - keep * tau[c, i])
            put_plane(fnat.at[c], i, n, end * (1.0 / COARSE))
    pairs = []
    for b in range(blocks):
        both = pl.ds(0, 2)
        pairs.append((fnat.at[both, b, pl.ds(EDGE, rows), :], fwd_ref.at[both, :, cut(b)]))
    started = copies(pairs, sem)
    for c in range(2):
        for p in range(GROUP):
            at = EDGE - HALO + (p % SPLIT) * STRIP
            tau_ref[p, c] = nat[c, :, at : at + WINDOW, :]
    for copy in started:
        copy.wait()


def chain_kernel(stage, stages, *refs):
    refs = list(refs)
    where_ref, tau_ref, nwin_ref = refs[:3]
    pieces = refs[3:6] if stage > 0 else None
    scratch = refs[-6:]
    nat, w, mid, cc, part, sem = scratch
    corr_ref, last_ref = refs[-8:-6]
    n = WINDOW // 8
    position = where_ref[0]
    planes = GROUP // SPLIT

    @pl.when(position // SPLIT == (stage + 1) * planes - 1)
    def _():
        coef = [cc.at[i] for i in range(4)]
        make_coefs(load_planes(nwin_ref, n), coarse_size, coef)

        def keep(t):
            for c in range(2):
                for i in range(n):
                    put_plane(nat.at[c], i, n, w[c, i])
                part[t, c] = nat[c, :, HALO : HALO + STRIP, :]

        def one(t):
            heun(w, mid, w, coef, n, lambda c, i: plane(tau_ref.at[t, c], i, n))
            keep(t + 1)

        if stage == 0:
            for c in range(2):
                part[0, c] = jnp.zeros_like(part[0, c])
                for i in range(n):
                    w[c, i] = plane(tau_ref.at[0, c], i, n)
            keep(1)
        else:
            for c in range(2):
                for k, ref in enumerate(pieces):
                    nat[c, :, k * STRIP : (k + 1) * STRIP, :] = ref[c]
                part[0, c] = pieces[1][c]
                for i in range(n):
                    w[c, i] = plane(nat.at[c], i, n)
            one(0)

        def step(t, carry):
            one(t)
            return carry

        lax.fori_loop(1, GROUP - 1, step, 0)
        copy = pltpu.make_async_copy(part.at[pl.ds(0, GROUP)], corr_ref, sem)
        copy.start()
        if stage + 1 < stages:
            one(GROUP - 1)
            last_ref[...] = part[GROUP]
        copy.wait()


def final_kernel(where_ref, got_ref, lo_ref, hi_ref, c_ref, clo_ref, chi_ref,
                 n_ref, handed_ref, handed2_ref,
                 corr_ref, adv_ref, defect_ref,
                 nat, vnat, anat, dbuf, w, mid, cf, sem):
    n = 12
    rows = n_ref.shape[0]
    blocks = nat.shape[1]
    position = where_ref[0]
    for b in range(blocks):
        vnat[b, 0:HALO, :] = clo_ref[2, EDGE - HALO :, b * LANES : (b + 1) * LANES]
        vnat[b, HALO : HALO + rows, :] = n_ref[:, b * LANES : (b + 1) * LANES]
        vnat[b, HALO + rows :, :] = chi_ref[2, 0:HALO, b * LANES : (b + 1) * LANES]
    coef = [cf.at[i] for i in range(4)]
    make_coefs(load_planes(vnat, n), coarse_size / STEPS, coef)

    @pl.when(position == 0)
    def _():
        for c in range(2):
            dbuf[c] = jnp.zeros_like(dbuf[c])
            for b in range(blocks):
                own = slice(b * LANES, (b + 1) * LANES)
                nat[c, b, 0:HALO, :] = clo_ref[c, EDGE - HALO :, own]
                nat[c, b, HALO : HALO + rows, :] = c_ref[0, c, :, own]
                nat[c, b, HALO + rows :, :] = chi_ref[c, 0:HALO, own]

    @pl.when(position != 0)
    def _():
        back = 1.0 / COARSE
        for c in range(2):
            dbuf[c] = (handed_ref[c] + handed2_ref[c]) - c_ref[0, c]
            nat[c, :, 0:HALO, :] = back * lo_ref[c]
            nat[c, :, HALO + rows :, :] = back * hi_ref[c]
            for q in range(SPLIT):
                at = HALO + q * STRIP
                nat[c, :, at : at + STRIP, :] = back * got_ref[GROUP - SPLIT + q, c]

    both = pl.ds(0, 2)
    mine = pl.ds(HALO, rows)
    pairs = [(dbuf, defect_ref.at[0])]
    for b in range(blocks):
        pairs.append((nat.at[both, b, mine, :], corr_ref.at[0, both, :, cut(b)]))
    started = copies(pairs, sem)
    for c in range(2):
        for i in range(n):
            w[c, i] = FINE * plane(nat.at[c], i, n)

    def step(_, carry):
        heun(w, mid, w, coef, n)
        return carry

    lax.fori_loop(0, STEPS, step, 0)
    for c in range(2):
        for i in range(n):
            put_plane(anat.at[c], i, n, w[c, i] * (1.0 / FINE))
    pairs = []
    for b in range(blocks):
        pairs.append((anat.at[both, b, mine, :], adv_ref.at[0, both, :, cut(b)]))
    started += copies(pairs, sem.at[pl.ds(1 + blocks, blocks)])
    for copy in started:
        copy.wait()


VMEM = pl.BlockSpec(memory_space=pltpu.VMEM)
SMEM = pl.BlockSpec(memory_space=pltpu.SMEM)
ANY = pl.BlockSpec(memory_space=pl.ANY)
HBM = pl.BlockSpec(memory_space=pltpu.HBM)
FULL = pltpu.CompilerParams(vmem_limit_bytes=63 * 1024 * 1024)
PARAMS = pltpu.CompilerParams(vmem_limit_bytes=48 * 1024 * 1024)


def shards(c_values, viscosity):
    _, _, rows, cols = c_values.shape
    blocks = cols // LANES
    ring = lax.axis_size("space")
    intervals = lax.axis_size("tm")
    stages = intervals // GROUP
    up = [(i, (i + 1) % ring) for i in range(ring)]
    down = [(b, a) for a, b in up]
    where = lax.axis_index("tm").reshape(1).astype(jnp.int32)
    shape = lambda *s: jax.ShapeDtypeStruct(s, f32)
    vm = lambda *s: pltpu.VMEM(s, f32)
    dma = lambda k: pltpu.SemaphoreType.DMA((k,))

    top, bottom = pl.pallas_call(
        edges_kernel,
        out_shape=(shape(3, EDGE, cols),) * 2,
        in_specs=[HBM] * 2,
        out_specs=(ANY,) * 2,
        scratch_shapes=[vm(2, 3, EDGE, cols), dma(8)],
        compiler_params=FULL,
        name="edges",
    )(c_values, viscosity)
    own = pl.pallas_call(
        load_kernel,
        out_shape=shape(3, rows, cols),
        in_specs=[ANY] * 2,
        out_specs=ANY,
        scratch_shapes=[dma(2)],
        compiler_params=PARAMS,
        cost_estimate=pl.CostEstimate(flops=0, bytes_accessed=6 * rows * cols * 4, transcendentals=0),
        name="load",
    )(c_values, viscosity)
    lo = lax.ppermute(bottom, "space", up)
    hi = lax.ppermute(top, "space", down)

    n = 16
    forward, tau, nwin = pl.pallas_call(
        forward_kernel,
        out_shape=(shape(2, rows, cols), shape(GROUP, 2, blocks, WINDOW, LANES), shape(blocks, WINDOW, LANES)),
        in_specs=[SMEM, ANY, ANY, ANY],
        out_specs=(HBM, VMEM, VMEM),
        scratch_shapes=[
            vm(3, blocks, 128, LANES), vm(2, blocks, 128, LANES),
            vm(2, n, 8, cols), vm(2, n, 8, cols), vm(2, n, 8, cols),
            vm(4, n + 1, 8, cols), vm(4, n + 1, 8, cols), dma(6 * blocks),
        ],
        compiler_params=PARAMS,
        name="forward",
    )(where, own, lo, hi)

    groups = [[g * GROUP + j for j in range(GROUP)] for g in range(stages)]
    taus = lax.all_to_all(tau, "tm", 0, 0, axis_index_groups=groups)

    strips = ring * SPLIT
    n = WINDOW // 8
    pieces, corr, handed = [], [], []
    for stage in range(stages):
        extra = {0: [forward], 1: handed, stages - 2: [forward], stages - 1: handed}[stage]
        carries = stage in (0, stages - 2)
        count = 3 + len(pieces)
        aliases = {count: 1} if stage > 0 else {}
        if carries:
            aliases[count + len(corr)] = 0
        kept = shape(2, rows, cols) if carries else shape(8, LANES)
        done = pl.pallas_call(
            functools.partial(chain_kernel, stage, stages),
            out_shape=(kept, shape(GROUP, 2, blocks, STRIP, LANES), shape(2, blocks, STRIP, LANES)),
            in_specs=[SMEM] + [VMEM] * (count - 1) + [ANY] * len(corr) + [HBM] * len(extra),
            out_specs=(HBM, ANY, VMEM),
            scratch_shapes=[
                vm(2, blocks, WINDOW, LANES), vm(2, n, 8, cols), vm(2, n, 8, cols), vm(4, n + 1, 8, cols),
                vm(GROUP + 1, 2, blocks, STRIP, LANES), pltpu.SemaphoreType.DMA,
            ],
            input_output_aliases=aliases,
            compiler_params=PARAMS,
            name="chain%d" % stage,
        )(where, taus, nwin, *pieces, *corr, *extra)
        corr, last = [done[1]], done[2]
        if carries:
            forward = done[0]
            chain = [g * GROUP + GROUP - 1 - q for g in range(2) for q in range(SPLIT)]
            pairs = [(i, i + 1) for i in range(intervals - 1) if (i in chain or i + 1 in chain) == (stage > 0)]
            handed = handed + [lax.ppermute(forward, "tm", pairs)]
        if stage + 1 < stages:
            pieces = []
            for delta in (1, 0, -1):
                pairs = []
                for strip in range(strips):
                    to = (strip + delta) % strips
                    source = stage * GROUP + GROUP - SPLIT + strip % SPLIT
                    target = (stage + 1) * GROUP + GROUP - SPLIT + to % SPLIT
                    pairs.append((source * ring + strip // SPLIT, target * ring + to // SPLIT))
                pieces.append(lax.ppermute(last, ("tm", "space"), pairs))

    got = lax.all_to_all(corr[0], "tm", 0, 0, axis_index_groups=groups)
    above = lax.ppermute(got[GROUP - 1], "space", up)
    below = lax.ppermute(got[GROUP - SPLIT], "space", down)

    n = 12
    return pl.pallas_call(
        final_kernel,
        out_shape=(shape(1, 2, rows, cols),) * 3,
        in_specs=[SMEM] + [VMEM] * 9,
        out_specs=(ANY,) * 3,
        scratch_shapes=[
            vm(2, blocks, 96, LANES), vm(blocks, 96, LANES), vm(2, blocks, 96, LANES), vm(2, rows, cols),
            vm(2, n, 8, cols), vm(2, n, 8, cols), vm(4, n + 1, 8, cols), dma(1 + 2 * blocks),
        ],
        compiler_params=PARAMS,
        name="final",
    )(where, got, above, below, c_values, lo, hi, viscosity, *handed)


def solution(mesh):
    return jax.shard_map(
        shards,
        mesh=mesh,
        in_specs=(P("tm", None, "space", None), P("space", None)),
        out_specs=(P("tm", None, "space", None),) * 3,
        check_vma=False,
    )
```

```python
import functools

import jax
import jax.numpy as jnp
from jax import lax
from jax.experimental import pallas as pl
from jax.experimental.pallas import tpu as pltpu
from jax.sharding import PartitionSpec as P

STEPS = 8
GROUP = 8
STRIP = 16
HALO = 16
EDGE = 32
WINDOW = STRIP + 2 * HALO
INNER = 8
LANES = 128
SPLIT = 4
advect_scale = 0.1
coarse_size = 1.0
COARSE = 0.5 * advect_scale * coarse_size
FINE = COARSE / STEPS
f32 = jnp.float32


def shift_up(plane):
    return pltpu.roll(plane, 1, 0)


def shift_down(plane):
    return pltpu.roll(plane, plane.shape[0] - 1, 0)


def left_of(x):
    return pltpu.roll(x, 1, 1)


def right_of(x):
    return pltpu.roll(x, x.shape[1] - 1, 1)


def make_coefs(planes, size, coef):
    cx, cyp, cym, dd = coef
    n = len(planes)
    faces = []
    for i in range(n):
        below = planes[i + 1] if i + 1 < n else shift_down(planes[0])
        faces.append((0.5 * size) * (planes[i] + below))
    first = shift_up(faces[n - 1])
    cx[0] = first
    for i in range(n):
        cx[i + 1] = faces[i]
        nyp = (0.5 * size) * (planes[i] + right_of(planes[i]))
        nym = left_of(nyp)
        cyp[i] = nyp
        cym[i] = nym
        nxm = faces[i - 1] if i > 0 else first
        dd[i] = 1.0 - ((faces[i] + nxm) + (nyp + nym))


def euler(src, coef, n, emit):
    cx, cyp, cym, dd = coef
    above = [shift_up(src[c, n - 1]) for c in range(2)]
    here = [src[c, 0] for c in range(2)]
    first = here
    for i in range(n):
        if i + 1 < n:
            below = [src[c, i + 1] for c in range(2)]
        else:
            below = [shift_down(first[c]) for c in range(2)]
        wxp = cx[i + 1] - here[0]
        wxm = cx[i] + here[0]
        wyp = cyp[i] - here[1]
        wym = cym[i] + here[1]
        d = dd[i]
        res = []
        for c in range(2):
            f = here[c]
            res.append(
                (d * f + (wxp * below[c] + wxm * above[c]))
                + (wyp * right_of(f) + wym * left_of(f))
            )
        emit(i, res)
        above, here = here, below


def heun(src, mid, dst, coef, n, extra=None):
    def to_mid(i, res):
        for c in range(2):
            mid[c, i] = res[c]

    euler(src, coef, n, to_mid)

    def to_dst(i, res):
        for c in range(2):
            out = 0.5 * (src[c, i] + res[c])
            if extra is not None:
                out = out + extra(c, i)
            dst[c, i] = out

    euler(mid, coef, n, to_dst)


def plane(nat, i, n):
    return jnp.concatenate([nat[b, pl.ds(i, 8, stride=n), :] for b in range(nat.shape[0])], axis=1)


def put_plane(nat, i, n, value):
    for b in range(nat.shape[0]):
        nat[b, pl.ds(i, 8, stride=n), :] = value[:, b * LANES : (b + 1) * LANES]


def load_planes(nat, n):
    return [plane(nat, i, n) for i in range(n)]


def fill(nat, at, ref, start, count):
    for b in range(nat.shape[0]):
        nat[b, at : at + count, :] = ref[start : start + count, b * LANES : (b + 1) * LANES]


def copies(pairs, sem):
    started = [pltpu.make_async_copy(a, b, sem.at[i]) for i, (a, b) in enumerate(pairs)]
    for copy in started:
        copy.start()
    return started


def edges_kernel(c_ref, n_ref, top_ref, bottom_ref, held, sem):
    rows = n_ref.shape[0]
    pairs, later = [], []
    for k, (out, start) in enumerate(((top_ref, 0), (bottom_ref, rows - EDGE))):
        pairs.append((c_ref.at[0, :, pl.ds(start, EDGE), :], held.at[k, pl.ds(0, 2)]))
        pairs.append((n_ref.at[pl.ds(start, EDGE), :], held.at[k, 2]))
        later += [(held.at[k, pl.ds(0, 2)], out.at[pl.ds(0, 2)]), (held.at[k, 2], out.at[2])]
    started = copies(pairs, sem)
    sent = []
    for i, copy in enumerate(started):
        copy.wait()
        sent += copies([later[i]], sem.at[pl.ds(4 + i, 1)])
    for copy in sent:
        copy.wait()


def load_kernel(c_ref, n_ref, out_ref, sem):
    pairs = [(c_ref.at[0], out_ref.at[pl.ds(0, 2)]), (n_ref, out_ref.at[2])]
    for copy in copies(pairs, sem):
        copy.wait()


def cut(b):
    return pl.ds(b * LANES, LANES)


def forward_kernel(where_ref, own_ref, lo_ref, hi_ref,
                   fwd_ref, nwin_ref, own_tau, near1, near2, near3, far0, far1, far2, far3,
                   nat, fnat, w, mid, tau, cf, cc, sem):
    n = 16
    blocks = nat.shape[1]
    rows = own_ref.shape[1]
    for c in (2, 0, 1):
        fill(nat.at[c], 0, lo_ref.at[c], 0, EDGE)
        fill(nat.at[c], EDGE, own_ref.at[c], 0, rows)
        fill(nat.at[c], EDGE + rows, hi_ref.at[c], 0, EDGE)
    position = where_ref[0]
    vnat = nat.at[2]
    start = pl.multiple_of(lax.rem(position, SPLIT) * STRIP + HALO, 8)
    nwin_ref[...] = nat[2, :, pl.ds(start, WINDOW), :]
    visc = load_planes(vnat, n)
    coef_c = [cc.at[i] for i in range(4)]
    coef_f = [cf.at[i] for i in range(4)]
    make_coefs(visc, coarse_size, coef_c)
    for i in range(n + 1):
        cf[0, i] = cc[0, i] * (1.0 / STEPS)
    for i in range(n):
        cf[1, i] = cc[1, i] * (1.0 / STEPS)
        cf[2, i] = cc[2, i] * (1.0 / STEPS)
        cf[3, i] = cc[3, i] * (1.0 / STEPS) + (1.0 - 1.0 / STEPS)
    for c in range(2):
        for i in range(n):
            w[c, i] = COARSE * plane(nat.at[c], i, n)
    heun(w, mid, tau, coef_c, n)
    for c in range(2):
        for i in range(n):
            w[c, i] = w[c, i] * (FINE / COARSE)

    def step(_, carry):
        heun(w, mid, w, coef_f, n)
        return carry

    lax.fori_loop(0, STEPS, step, 0)
    keep = jnp.where(position == 0, 0.0, 1.0).astype(f32)
    for c in range(2):
        for i in range(n):
            end = w[c, i] * (COARSE / FINE)
            put_plane(nat.at[c], i, n, end - keep * tau[c, i])
            put_plane(fnat.at[c], i, n, end * (1.0 / COARSE))
    pairs = []
    for b in range(blocks):
        both = pl.ds(0, 2)
        pairs.append((fnat.at[both, b, pl.ds(EDGE, rows), :], fwd_ref.at[both, :, cut(b)]))
    started = copies(pairs, sem)
    for k, ref in enumerate((own_tau, near1, near2, near3)):
        first = lax.rem(position + k, SPLIT) * STRIP + (EDGE - HALO)
        ref[...] = nat[0:2, :, pl.ds(pl.multiple_of(first, 8), WINDOW), :]
    for k, ref in enumerate((far0, far1, far2, far3)):
        first = lax.rem(position + k, SPLIT) * STRIP + (EDGE - INNER)
        ref[...] = nat[0:2, :, pl.ds(pl.multiple_of(first, 8), STRIP + 2 * INNER), :]
    for copy in started:
        copy.wait()


def prep_kernel(nwin_ref, cc_ref):
    make_coefs(load_planes(nwin_ref, WINDOW // 8), coarse_size, [cc_ref.at[i] for i in range(4)])


def chain_kernel(stage, stages, carried, *refs):
    refs = list(refs)
    where_ref, cc_ref = refs[:2]
    nat, w, mid = refs[-3:]
    corr_ref, last_ref = refs[-5:-3]
    n = WINDOW // 8
    position = where_ref[0]
    planes = GROUP // SPLIT
    rest = refs[2 + carried :]
    if stage == 0:
        tau_ref = refs[-6]
        for k in range(SPLIT):
            source = lax.rem(position + SPLIT - k, SPLIT)
            tau_ref[source] = rest[k][...]
            far = source + SPLIT
            tau_ref[far, :, :, 0:INNER, :] = jnp.zeros_like(rest[0][:, :, 0:INNER, :])
            tau_ref[far, :, :, WINDOW - INNER :, :] = jnp.zeros_like(rest[0][:, :, 0:INNER, :])
            tau_ref[far, :, :, INNER : WINDOW - INNER, :] = rest[SPLIT + k][...]
    else:
        tau_ref = rest[0]
        own, above, below, corr_in = rest[1:5]
    active = position // SPLIT == stage * planes

    @pl.when(active)
    def _():
        coef = [cc_ref.at[i] for i in range(4)]

        def keep(out):
            for c in range(2):
                for i in range(n):
                    put_plane(nat.at[c], i, n, w[c, i])
                out[c] = nat[c, :, HALO : HALO + STRIP, :]

        def one(t, out):
            heun(w, mid, w, coef, n, lambda c, i: plane(tau_ref.at[t, c], i, n))
            keep(out)

        if stage == 0:
            for c in range(2):
                corr_ref[0, c] = jnp.zeros_like(corr_ref[0, c])
                for i in range(n):
                    w[c, i] = plane(tau_ref.at[0, c], i, n)
            keep(corr_ref.at[1])
        else:
            for c in range(2):
                for k, ref in enumerate((above, own, below)):
                    nat[c, :, k * STRIP : (k + 1) * STRIP, :] = ref[c]
                corr_ref[0, c] = own[c]
                for i in range(n):
                    w[c, i] = plane(nat.at[c], i, n)
            one(0, corr_ref.at[1])

        def step(t, carry):
            one(t, corr_ref.at[t + 1])
            return carry

        lax.fori_loop(1, GROUP - 1, step, 0)
        if stage + 1 < stages:
            one(GROUP - 1, last_ref)

    if stage > 0:

        @pl.when(jnp.logical_not(active))
        def _():
            corr_ref[...] = corr_in[...]


def final_kernel(where_ref, got_ref, lo_ref, hi_ref, c_ref, clo_ref, chi_ref,
                 n_ref, handed_ref, handed2_ref,
                 corr_ref, adv_ref, defect_ref,
                 nat, vnat, anat, dbuf, w, mid, cf, sem):
    n = 12
    rows = n_ref.shape[0]
    blocks = nat.shape[1]
    position = where_ref[0]
    fill(vnat, 0, clo_ref.at[2], EDGE - HALO, HALO)
    fill(vnat, HALO, n_ref, 0, rows)
    fill(vnat, HALO + rows, chi_ref.at[2], 0, HALO)
    coef = [cf.at[i] for i in range(4)]
    make_coefs(load_planes(vnat, n), coarse_size / STEPS, coef)

    @pl.when(position == 0)
    def _():
        for c in range(2):
            dbuf[c] = jnp.zeros_like(dbuf[c])
            for b in range(blocks):
                own = slice(b * LANES, (b + 1) * LANES)
                nat[c, b, 0:HALO, :] = clo_ref[c, EDGE - HALO :, own]
                nat[c, b, HALO : HALO + rows, :] = c_ref[0, c, :, own]
                nat[c, b, HALO + rows :, :] = chi_ref[c, 0:HALO, own]

    @pl.when(position != 0)
    def _():
        back = 1.0 / COARSE
        for c in range(2):
            dbuf[c] = (handed_ref[c] + handed2_ref[c]) - c_ref[0, c]
            nat[c, :, 0:HALO, :] = back * lo_ref[c]
            nat[c, :, HALO + rows :, :] = back * hi_ref[c]
            for q in range(SPLIT):
                at = HALO + q * STRIP
                nat[c, :, at : at + STRIP, :] = back * got_ref[q, c]

    both = pl.ds(0, 2)
    mine = pl.ds(HALO, rows)
    pairs = [(dbuf, defect_ref.at[0])]
    for b in range(blocks):
        pairs.append((nat.at[both, b, mine, :], corr_ref.at[0, both, :, cut(b)]))
    started = copies(pairs, sem)
    for c in range(2):
        for i in range(n):
            w[c, i] = FINE * plane(nat.at[c], i, n)

    def step(_, carry):
        heun(w, mid, w, coef, n)
        return carry

    lax.fori_loop(0, STEPS, step, 0)
    for c in range(2):
        for i in range(n):
            put_plane(anat.at[c], i, n, w[c, i] * (1.0 / FINE))
    pairs = []
    for b in range(blocks):
        pairs.append((anat.at[both, b, mine, :], adv_ref.at[0, both, :, cut(b)]))
    started += copies(pairs, sem.at[pl.ds(1 + blocks, blocks)])
    for copy in started:
        copy.wait()


VMEM = pl.BlockSpec(memory_space=pltpu.VMEM)
SMEM = pl.BlockSpec(memory_space=pltpu.SMEM)
ANY = pl.BlockSpec(memory_space=pl.ANY)
HBM = pl.BlockSpec(memory_space=pltpu.HBM)
FULL = pltpu.CompilerParams(vmem_limit_bytes=63 * 1024 * 1024)
PARAMS = pltpu.CompilerParams(vmem_limit_bytes=48 * 1024 * 1024)


def shards(c_values, viscosity):
    _, _, rows, cols = c_values.shape
    blocks = cols // LANES
    ring = lax.axis_size("space")
    intervals = lax.axis_size("tm")
    stages = intervals // GROUP
    up = [(i, (i + 1) % ring) for i in range(ring)]
    down = [(b, a) for a, b in up]
    where = lax.axis_index("tm").reshape(1).astype(jnp.int32)
    shape = lambda *s: jax.ShapeDtypeStruct(s, f32)
    vm = lambda *s: pltpu.VMEM(s, f32)
    dma = lambda k: pltpu.SemaphoreType.DMA((k,))

    top, bottom = pl.pallas_call(
        edges_kernel,
        out_shape=(shape(3, EDGE, cols),) * 2,
        in_specs=[HBM] * 2,
        out_specs=(ANY,) * 2,
        scratch_shapes=[vm(2, 3, EDGE, cols), dma(8)],
        compiler_params=FULL,
        name="edges",
    )(c_values, viscosity)
    own = pl.pallas_call(
        load_kernel,
        out_shape=shape(3, rows, cols),
        in_specs=[ANY] * 2,
        out_specs=ANY,
        scratch_shapes=[dma(2)],
        compiler_params=PARAMS,
        cost_estimate=pl.CostEstimate(flops=0, bytes_accessed=6 * rows * cols * 4, transcendentals=0),
        name="load",
    )(c_values, viscosity)
    lo = lax.ppermute(bottom, "space", up)
    hi = lax.ppermute(top, "space", down)

    n = 16
    window = shape(2, blocks, WINDOW, LANES)
    inner = shape(2, blocks, STRIP + 2 * INNER, LANES)
    forward, nwin, *sent = pl.pallas_call(
        forward_kernel,
        out_shape=(shape(2, rows, cols), shape(blocks, WINDOW, LANES)) + (window,) * SPLIT + (inner,) * SPLIT,
        in_specs=[SMEM, VMEM, VMEM, VMEM],
        out_specs=(HBM,) + (VMEM,) * (1 + 2 * SPLIT),
        scratch_shapes=[
            vm(3, blocks, 128, LANES), vm(2, blocks, 128, LANES),
            vm(2, n, 8, cols), vm(2, n, 8, cols), vm(2, n, 8, cols),
            vm(4, n + 1, 8, cols), vm(4, n + 1, 8, cols), dma(blocks),
        ],
        compiler_params=PARAMS,
        name="forward",
    )(where, own, lo, hi)

    n = WINDOW // 8
    cc = pl.pallas_call(
        prep_kernel,
        out_shape=shape(4, n + 1, 8, cols),
        in_specs=[VMEM],
        out_specs=VMEM,
        compiler_params=PARAMS,
        name="prep",
    )(nwin)

    planes = range(0, intervals, SPLIT)
    gathered = [sent[0]]
    for k in range(1, SPLIT):
        pairs = [(p + q, p + (q + k) % SPLIT) for p in planes for q in range(SPLIT)]
        gathered.append(lax.ppermute(sent[k], "tm", pairs))
    for k in range(SPLIT):
        pairs = []
        for p in range(0, intervals, GROUP):
            for q in range(SPLIT):
                a, b = p + SPLIT + q, p + (q + k) % SPLIT
                pairs += [(a, b), (b, a)]
        gathered.append(lax.ppermute(sent[SPLIT + k], "tm", pairs))
    groups = [[g * GROUP + j for j in range(GROUP)] for g in range(stages)]

    strips = ring * SPLIT
    pieces, corr, handed = [], [], []
    for stage in range(stages):
        extra = {0: [forward], 1: handed, stages - 2: [forward], stages - 1: handed}[stage]
        carries = stage in (0, stages - 2)
        operands = [where, cc] + extra + (gathered if stage == 0 else [taus] + pieces + corr)
        specs = [SMEM, VMEM] + [HBM] * len(extra) + [VMEM] * (len(operands) - 2 - len(extra))
        shapes = [shape(2, rows, cols) if carries else shape(8, LANES)]
        shapes += [shape(GROUP, 2, blocks, WINDOW, LANES)] if stage == 0 else []
        shapes += [shape(GROUP, 2, blocks, STRIP, LANES), shape(2, blocks, STRIP, LANES)]
        aliases = {len(operands) - 1: 1} if stage > 0 else {}
        if carries:
            aliases[2] = 0
        done = pl.pallas_call(
            functools.partial(chain_kernel, stage, stages, len(extra)),
            out_shape=tuple(shapes),
            in_specs=specs,
            out_specs=(HBM,) + (VMEM,) * (len(shapes) - 1),
            scratch_shapes=[vm(2, blocks, WINDOW, LANES), vm(2, n, 8, cols), vm(2, n, 8, cols)],
            input_output_aliases=aliases,
            compiler_params=PARAMS,
            name="chain%d" % stage,
        )(*operands)
        if stage == 0:
            taus = done[1]
        corr, last = [done[-2]], done[-1]
        if carries:
            forward = done[0]
            chain = [g * GROUP + q for g in range(2) for q in range(SPLIT)]
            pairs = [(i, i + 1) for i in range(intervals - 1) if (i in chain or i + 1 in chain) == (stage > 0)]
            handed = handed + [lax.ppermute(forward, "tm", pairs)]
        if stage + 1 < stages:
            arrived = {}
            for delta in (0, 1, -1):
                pairs = []
                for strip in range(strips):
                    to = (strip + delta) % strips
                    source = stage * GROUP + strip % SPLIT
                    target = (stage + 1) * GROUP + to % SPLIT
                    pairs.append((source * ring + strip // SPLIT, target * ring + to // SPLIT))
                arrived[delta] = lax.ppermute(last, ("tm", "space"), pairs)
            pieces = [arrived[0], arrived[1], arrived[-1]]

    got = lax.all_to_all(corr[0], "tm", 0, 0, axis_index_groups=groups)
    above = lax.ppermute(got[SPLIT - 1], "space", up)
    below = lax.ppermute(got[0], "space", down)

    n = 12
    return pl.pallas_call(
        final_kernel,
        out_shape=(shape(1, 2, rows, cols),) * 3,
        in_specs=[SMEM] + [VMEM] * 9,
        out_specs=(ANY,) * 3,
        scratch_shapes=[
            vm(2, blocks, 8 * n, LANES), vm(blocks, 8 * n, LANES), vm(2, blocks, 8 * n, LANES), vm(2, rows, cols),
            vm(2, n, 8, cols), vm(2, n, 8, cols), vm(4, n + 1, 8, cols), dma(1 + 2 * blocks),
        ],
        compiler_params=PARAMS,
        name="final",
    )(where, got, above, below, c_values, lo, hi, viscosity, *handed)


def solution(mesh):
    return jax.shard_map(
        shards,
        mesh=mesh,
        in_specs=(P("tm", None, "space", None), P("space", None)),
        out_specs=(P("tm", None, "space", None),) * 3,
        check_vma=False,
    )
```

```python
import functools

import jax
import jax.numpy as jnp
from jax import lax
from jax.experimental import pallas as pl
from jax.experimental.pallas import tpu as pltpu
from jax.sharding import PartitionSpec as P

STEPS = 8
GROUP = 8
STRIP = 16
HALO = 16
EDGE = 32
WINDOW = STRIP + 2 * HALO
INNER = 8
TIGHT = STRIP + 2 * INNER
FINAL = 96
LANES = 128
SPLIT = 4
advect_scale = 0.1
coarse_size = 1.0
COARSE = 0.5 * advect_scale * coarse_size
FINE = COARSE / STEPS
f32 = jnp.float32


def shift_up(plane):
    return pltpu.roll(plane, 1, 0)


def shift_down(plane):
    return pltpu.roll(plane, plane.shape[0] - 1, 0)


def left_of(x):
    return pltpu.roll(x, 1, 1)


def right_of(x):
    return pltpu.roll(x, x.shape[1] - 1, 1)


def make_coefs(planes, size, coef):
    cx, cyp, cym, dd = coef
    n = len(planes)
    faces = []
    for i in range(n):
        below = planes[i + 1] if i + 1 < n else shift_down(planes[0])
        faces.append((0.5 * size) * (planes[i] + below))
    first = shift_up(faces[n - 1])
    cx[0] = first
    for i in range(n):
        cx[i + 1] = faces[i]
        nyp = (0.5 * size) * (planes[i] + right_of(planes[i]))
        nym = left_of(nyp)
        cyp[i] = nyp
        cym[i] = nym
        nxm = faces[i - 1] if i > 0 else first
        dd[i] = 1.0 - ((faces[i] + nxm) + (nyp + nym))


def euler(src, coef, n, emit):
    cx, cyp, cym, dd = coef
    above = [shift_up(src[c, n - 1]) for c in range(2)]
    here = [src[c, 0] for c in range(2)]
    first = here
    for i in range(n):
        if i + 1 < n:
            below = [src[c, i + 1] for c in range(2)]
        else:
            below = [shift_down(first[c]) for c in range(2)]
        wxp = cx[i + 1] - here[0]
        wxm = cx[i] + here[0]
        wyp = cyp[i] - here[1]
        wym = cym[i] + here[1]
        d = dd[i]
        res = []
        for c in range(2):
            f = here[c]
            res.append(
                (d * f + (wxp * below[c] + wxm * above[c]))
                + (wyp * right_of(f) + wym * left_of(f))
            )
        emit(i, res)
        above, here = here, below


def heun(src, mid, dst, coef, n, extra=None):
    def to_mid(i, res):
        for c in range(2):
            mid[c, i] = res[c]

    euler(src, coef, n, to_mid)

    def to_dst(i, res):
        for c in range(2):
            out = 0.5 * (src[c, i] + res[c])
            if extra is not None:
                out = out + extra(c, i)
            dst[c, i] = out

    euler(mid, coef, n, to_dst)


def plane(nat, i, n, first=0):
    return jnp.concatenate(
        [nat[b, pl.ds(first + i, 8, stride=n), :] for b in range(nat.shape[0])], axis=1
    )


def put_plane(nat, i, n, value):
    for b in range(nat.shape[0]):
        nat[b, pl.ds(i, 8, stride=n), :] = value[:, b * LANES : (b + 1) * LANES]


def load_planes(nat, n, first=0):
    return [plane(nat, i, n, first) for i in range(n)]


def fill(nat, at, ref, start, count):
    for b in range(nat.shape[0]):
        nat[b, at : at + count, :] = ref[start : start + count, b * LANES : (b + 1) * LANES]


def copies(pairs, sem):
    started = [pltpu.make_async_copy(a, b, sem.at[i]) for i, (a, b) in enumerate(pairs)]
    for copy in started:
        copy.start()
    return started


def edges_kernel(c_ref, n_ref, top_ref, bottom_ref, held, sem):
    rows = n_ref.shape[0]
    pairs, later = [], []
    for k, (out, start) in enumerate(((top_ref, 0), (bottom_ref, rows - EDGE))):
        pairs.append((c_ref.at[0, :, pl.ds(start, EDGE), :], held.at[k, pl.ds(0, 2)]))
        pairs.append((n_ref.at[pl.ds(start, EDGE), :], held.at[k, 2]))
        later += [(held.at[k, pl.ds(0, 2)], out.at[pl.ds(0, 2)]), (held.at[k, 2], out.at[2])]
    started = copies(pairs, sem)
    sent = []
    for i, copy in enumerate(started):
        copy.wait()
        sent += copies([later[i]], sem.at[pl.ds(4 + i, 1)])
    for copy in sent:
        copy.wait()


def load_kernel(c_ref, n_ref, out_ref, sem):
    pairs = [(c_ref.at[0], out_ref.at[pl.ds(0, 2)]), (n_ref, out_ref.at[2])]
    for copy in copies(pairs, sem):
        copy.wait()


def cut(b):
    return pl.ds(b * LANES, LANES)


def forward_kernel(where_ref, own_ref, lo_ref, hi_ref,
                   fwd_ref, nwin_ref, own_tau, near1, near2, near3, far0, far1, far2, far3,
                   nat, fnat, w, mid, tau, cf, cc, sem):
    n = 16
    blocks = nat.shape[1]
    rows = own_ref.shape[1]
    for c in (2, 0, 1):
        fill(nat.at[c], 0, lo_ref.at[c], 0, EDGE)
        fill(nat.at[c], EDGE, own_ref.at[c], 0, rows)
        fill(nat.at[c], EDGE + rows, hi_ref.at[c], 0, EDGE)
    position = where_ref[0]
    vnat = nat.at[2]
    start = pl.multiple_of(lax.rem(position, SPLIT) * STRIP + HALO, 8)
    nwin_ref[...] = nat[2, :, pl.ds(start, WINDOW), :]
    visc = load_planes(vnat, n)
    coef_c = [cc.at[i] for i in range(4)]
    coef_f = [cf.at[i] for i in range(4)]
    make_coefs(visc, coarse_size, coef_c)
    for i in range(n + 1):
        cf[0, i] = cc[0, i] * (1.0 / STEPS)
    for i in range(n):
        cf[1, i] = cc[1, i] * (1.0 / STEPS)
        cf[2, i] = cc[2, i] * (1.0 / STEPS)
        cf[3, i] = cc[3, i] * (1.0 / STEPS) + (1.0 - 1.0 / STEPS)
    for c in range(2):
        for i in range(n):
            w[c, i] = COARSE * plane(nat.at[c], i, n)
    heun(w, mid, tau, coef_c, n)
    for c in range(2):
        for i in range(n):
            w[c, i] = w[c, i] * (FINE / COARSE)

    def step(_, carry):
        heun(w, mid, w, coef_f, n)
        return carry

    lax.fori_loop(0, STEPS, step, 0)
    keep = jnp.where(position == 0, 0.0, 1.0).astype(f32)
    for c in range(2):
        for i in range(n):
            end = w[c, i] * (COARSE / FINE)
            put_plane(nat.at[c], i, n, end - keep * tau[c, i])
            put_plane(fnat.at[c], i, n, end * (1.0 / COARSE))
    pairs = []
    for b in range(blocks):
        both = pl.ds(0, 2)
        pairs.append((fnat.at[both, b, pl.ds(EDGE, rows), :], fwd_ref.at[both, :, cut(b)]))
    started = copies(pairs, sem)
    for k, ref in enumerate((own_tau, near1, near2, near3)):
        first = lax.rem(position + k, SPLIT) * STRIP + (EDGE - HALO)
        ref[...] = nat[0:2, :, pl.ds(pl.multiple_of(first, 8), WINDOW), :]
    for k, ref in enumerate((far0, far1, far2, far3)):
        first = lax.rem(position + k, SPLIT) * STRIP + (EDGE - INNER)
        ref[...] = nat[0:2, :, pl.ds(pl.multiple_of(first, 8), TIGHT), :]
    for copy in started:
        copy.wait()


def prep_kernel(nwin_ref, wide_ref, tight_ref):
    wide = [wide_ref.at[i] for i in range(4)]
    tight = [tight_ref.at[i] for i in range(4)]
    make_coefs(load_planes(nwin_ref, WINDOW // 8), coarse_size, wide)
    make_coefs(load_planes(nwin_ref, TIGHT // 8, HALO - INNER), coarse_size, tight)


def chain_kernel(stage, stages, carried, *refs):
    refs = list(refs)
    where_ref, wide_ref, tight_ref = refs[:3]
    nat, w, mid, nat_t, w_t, mid_t = refs[-6:]
    if stage + 1 < stages:
        last_ref = refs.pop(-7)
    corr_ref = refs[-7]
    n, n_t = WINDOW // 8, TIGHT // 8
    position = where_ref[0]
    planes = GROUP // SPLIT
    rest = refs[3 + carried :]
    if stage == 0:
        near_ref, far_ref = refs[-9:-7]
        for k in range(SPLIT):
            source = lax.rem(position + SPLIT - k, SPLIT)
            near_ref[source] = rest[k][...]
            far_ref[source] = rest[SPLIT + k][...]
    else:
        near_ref, far_ref, own, pair, other, corr_in = rest[:6]
    active = position // SPLIT == stage * planes

    @pl.when(active)
    def _():
        wide = [wide_ref.at[i] for i in range(4)]
        tight = [tight_ref.at[i] for i in range(4)]

        def keep(out):
            for c in range(2):
                for i in range(n):
                    put_plane(nat.at[c], i, n, w[c, i])
                out[c] = nat[c, :, HALO : HALO + STRIP, :]

        def one(t, out):
            heun(w, mid, w, wide, n, lambda c, i: plane(near_ref.at[t, c], i, n))
            keep(out)

        def one_tight(t, out):
            heun(w_t, mid_t, w_t, tight, n_t, lambda c, i: plane(far_ref.at[t - SPLIT, c], i, n_t))
            for c in range(2):
                for i in range(n_t):
                    put_plane(nat_t.at[c], i, n_t, w_t[c, i])
                out[c] = nat_t[c, :, INNER : INNER + STRIP, :]

        if stage == 0:
            for c in range(2):
                corr_ref[0, c] = jnp.zeros_like(corr_ref[0, c])
                for i in range(n):
                    w[c, i] = plane(near_ref.at[0, c], i, n)
            keep(corr_ref.at[1])
        else:
            even = lax.rem(position, 2) == 0
            for choice, refs_in_order in ((even, (other, own, pair)), (jnp.logical_not(even), (pair, own, other))):

                @pl.when(choice)
                def _():
                    for c in range(2):
                        for k, ref in enumerate(refs_in_order):
                            nat[c, :, k * STRIP : (k + 1) * STRIP, :] = ref[c]

            for c in range(2):
                corr_ref[0, c] = own[c]
                for i in range(n):
                    w[c, i] = plane(nat.at[c], i, n)
            one(0, corr_ref.at[1])

        def step(t, carry):
            one(t, corr_ref.at[t + 1])
            return carry

        def step_tight(t, carry):
            one_tight(t, corr_ref.at[t + 1])
            return carry

        lax.fori_loop(1, SPLIT, step, 0)
        for c in range(2):
            for i in range(n_t):
                w_t[c, i] = plane(nat.at[c], i, n_t, HALO - INNER)
        lax.fori_loop(SPLIT, GROUP - 1, step_tight, 0)
        if stage + 1 < stages:
            one_tight(GROUP - 1, last_ref)

    if stage > 0:

        @pl.when(jnp.logical_not(active))
        def _():
            corr_ref[...] = corr_in[...]


def ready_kernel(where_ref, got_ref, c_ref, clo_ref, chi_ref, n_ref, handed_ref, handed2_ref,
                 corr_ref, defect_ref, own_ref, cf_ref,
                 vnat, dbuf, sem):
    n = FINAL // 8
    rows = n_ref.shape[0]
    blocks = vnat.shape[0]
    position = where_ref[0]

    @pl.when(position == 0)
    def _():
        for c in range(2):
            dbuf[c] = jnp.zeros_like(dbuf[c])
            fill(own_ref.at[c], 0, c_ref.at[0, c], 0, rows)

    @pl.when(position != 0)
    def _():
        back = 1.0 / COARSE
        for c in range(2):
            dbuf[c] = (handed_ref[c] + handed2_ref[c]) - c_ref[0, c]
            for q in range(SPLIT):
                own_ref[c, :, q * STRIP : (q + 1) * STRIP, :] = back * got_ref[q, c]

    both = pl.ds(0, 2)
    pairs = [(dbuf, defect_ref.at[0])]
    for b in range(blocks):
        pairs.append((own_ref.at[both, b], corr_ref.at[0, both, :, cut(b)]))
    started = copies(pairs, sem)
    fill(vnat, 0, clo_ref.at[2], EDGE - HALO, HALO)
    fill(vnat, HALO, n_ref, 0, rows)
    fill(vnat, HALO + rows, chi_ref.at[2], 0, HALO)
    make_coefs(load_planes(vnat, n), coarse_size / STEPS, [cf_ref.at[i] for i in range(4)])
    for copy in started:
        copy.wait()


def final_kernel(where_ref, own_ref, lo_ref, hi_ref, clo_ref, chi_ref, cf_ref,
                 adv_ref,
                 nat, anat, w, mid, sem):
    n = FINAL // 8
    rows = own_ref.shape[2]
    blocks = nat.shape[1]
    position = where_ref[0]
    coef = [cf_ref.at[i] for i in range(4)]

    @pl.when(position == 0)
    def _():
        for c in range(2):
            fill(nat.at[c], 0, clo_ref.at[c], EDGE - HALO, HALO)
            fill(nat.at[c], HALO + rows, chi_ref.at[c], 0, HALO)

    @pl.when(position != 0)
    def _():
        back = 1.0 / COARSE
        for c in range(2):
            nat[c, :, 0:HALO, :] = back * lo_ref[c]
            nat[c, :, HALO + rows :, :] = back * hi_ref[c]

    both = pl.ds(0, 2)
    mine = pl.ds(HALO, rows)
    for c in range(2):
        nat[c, :, HALO : HALO + rows, :] = own_ref[c]
        for i in range(n):
            w[c, i] = FINE * plane(nat.at[c], i, n)

    def step(_, carry):
        heun(w, mid, w, coef, n)
        return carry

    lax.fori_loop(0, STEPS, step, 0)
    started = []
    for b in range(blocks):
        for c in range(2):
            for i in range(n):
                part = w[c, i, :, b * LANES : (b + 1) * LANES]
                anat[c, b, pl.ds(i, 8, stride=n), :] = part * (1.0 / FINE)
        pair = (anat.at[both, b, mine, :], adv_ref.at[0, both, :, cut(b)])
        started += copies([pair], sem.at[pl.ds(b, 1)])
    for copy in started:
        copy.wait()


VMEM = pl.BlockSpec(memory_space=pltpu.VMEM)
SMEM = pl.BlockSpec(memory_space=pltpu.SMEM)
ANY = pl.BlockSpec(memory_space=pl.ANY)
HBM = pl.BlockSpec(memory_space=pltpu.HBM)
FULL = pltpu.CompilerParams(vmem_limit_bytes=63 * 1024 * 1024)
PARAMS = pltpu.CompilerParams(vmem_limit_bytes=48 * 1024 * 1024)


def shards(c_values, viscosity):
    _, _, rows, cols = c_values.shape
    blocks = cols // LANES
    ring = lax.axis_size("space")
    intervals = lax.axis_size("tm")
    stages = intervals // GROUP
    up = [(i, (i + 1) % ring) for i in range(ring)]
    down = [(b, a) for a, b in up]
    where = lax.axis_index("tm").reshape(1).astype(jnp.int32)
    shape = lambda *s: jax.ShapeDtypeStruct(s, f32)
    vm = lambda *s: pltpu.VMEM(s, f32)
    dma = lambda k: pltpu.SemaphoreType.DMA((k,))

    top, bottom = pl.pallas_call(
        edges_kernel,
        out_shape=(shape(3, EDGE, cols),) * 2,
        in_specs=[HBM] * 2,
        out_specs=(ANY,) * 2,
        scratch_shapes=[vm(2, 3, EDGE, cols), dma(8)],
        compiler_params=FULL,
        name="edges",
    )(c_values, viscosity)
    own = pl.pallas_call(
        load_kernel,
        out_shape=shape(3, rows, cols),
        in_specs=[ANY] * 2,
        out_specs=ANY,
        scratch_shapes=[dma(2)],
        compiler_params=PARAMS,
        cost_estimate=pl.CostEstimate(flops=0, bytes_accessed=6 * rows * cols * 4, transcendentals=0),
        name="load",
    )(c_values, viscosity)
    lo = lax.ppermute(bottom, "space", up)
    hi = lax.ppermute(top, "space", down)

    n = 16
    window = shape(2, blocks, WINDOW, LANES)
    inner = shape(2, blocks, TIGHT, LANES)
    forward, nwin, *sent = pl.pallas_call(
        forward_kernel,
        out_shape=(shape(2, rows, cols), shape(blocks, WINDOW, LANES)) + (window,) * SPLIT + (inner,) * SPLIT,
        in_specs=[SMEM, VMEM, VMEM, VMEM],
        out_specs=(HBM,) + (VMEM,) * (1 + 2 * SPLIT),
        scratch_shapes=[
            vm(3, blocks, 128, LANES), vm(2, blocks, 128, LANES),
            vm(2, n, 8, cols), vm(2, n, 8, cols), vm(2, n, 8, cols),
            vm(4, n + 1, 8, cols), vm(4, n + 1, 8, cols), dma(blocks),
        ],
        compiler_params=PARAMS,
        name="forward",
    )(where, own, lo, hi)

    n, n_t = WINDOW // 8, TIGHT // 8
    coefs = pl.pallas_call(
        prep_kernel,
        out_shape=(shape(4, n + 1, 8, cols), shape(4, n_t + 1, 8, cols)),
        in_specs=[VMEM],
        out_specs=(VMEM, VMEM),
        compiler_params=PARAMS,
        name="prep",
    )(nwin)

    planes = range(0, intervals, SPLIT)
    gathered = [sent[0]]
    for k in range(1, SPLIT):
        pairs = [(p + q, p + (q + k) % SPLIT) for p in planes for q in range(SPLIT)]
        gathered.append(lax.ppermute(sent[k], "tm", pairs))
    for k in range(SPLIT):
        pairs = []
        for p in range(0, intervals, GROUP):
            for q in range(SPLIT):
                a, b = p + SPLIT + q, p + (q + k) % SPLIT
                pairs += [(a, b), (b, a)]
        gathered.append(lax.ppermute(sent[SPLIT + k], "tm", pairs))
    groups = [[g * GROUP + j for j in range(GROUP)] for g in range(stages)]

    strips = ring * SPLIT
    pieces, handed = [], []
    for stage in range(stages):
        carries = stage in (0, stages - 2)
        extra = ([forward] if carries else []) + (handed if stage >= stages - 2 else [])
        operands = [where, *coefs] + extra + (gathered if stage == 0 else [*taus, *pieces, corr])
        specs = [SMEM, VMEM, VMEM] + [HBM] * len(extra) + [VMEM] * (len(operands) - 3 - len(extra))
        shapes = [shape(2, rows, cols) if carries else shape(8, LANES)]
        if stage == 0:
            shapes += [shape(SPLIT, 2, blocks, WINDOW, LANES), shape(SPLIT, 2, blocks, TIGHT, LANES)]
        shapes += [shape(GROUP, 2, blocks, STRIP, LANES)]
        shapes += [shape(2, blocks, STRIP, LANES)] if stage + 1 < stages else []
        aliases = {len(operands) - 1: 1} if stage > 0 else {}
        if carries:
            aliases[3] = 0
        done = pl.pallas_call(
            functools.partial(chain_kernel, stage, stages, len(extra)),
            out_shape=tuple(shapes),
            in_specs=specs,
            out_specs=(HBM,) + (VMEM,) * (len(shapes) - 1),
            scratch_shapes=[
                vm(2, blocks, WINDOW, LANES), vm(2, n, 8, cols), vm(2, n, 8, cols),
                vm(2, blocks, TIGHT, LANES), vm(2, n_t, 8, cols), vm(2, n_t, 8, cols),
            ],
            input_output_aliases=aliases,
            compiler_params=PARAMS,
            name="chain%d" % stage,
        )(*operands)
        if stage == 0:
            taus = done[1:3]
        corr, last = done[-2:] if stage + 1 < stages else (done[-1], None)
        if carries:
            forward = done[0]
            chain = [g * GROUP + q for g in range(2) for q in range(SPLIT)]
            pairs = [(i, i + 1) for i in range(intervals - 1) if (i in chain or i + 1 in chain) == (stage > 0)]
            handed = handed + [lax.ppermute(forward, "tm", pairs)]
        if stage + 1 < stages:
            pieces = []
            moves = (lambda q: q, lambda q: q + 1 - 2 * (q % 2), lambda q: (q - 1 + 2 * (q % 2)) % strips)
            for move in moves:
                pairs = []
                for strip in range(strips):
                    to = move(strip)
                    source = stage * GROUP + strip % SPLIT
                    target = (stage + 1) * GROUP + to % SPLIT
                    pairs.append((source * ring + strip // SPLIT, target * ring + to // SPLIT))
                pieces.append(lax.ppermute(last, ("tm", "space"), pairs))

    got = lax.all_to_all(corr, "tm", 0, 0, axis_index_groups=groups)
    above = lax.ppermute(got[SPLIT - 1], "space", up)
    below = lax.ppermute(got[0], "space", down)

    n = FINAL // 8
    corrected, defect, mine, cf = pl.pallas_call(
        ready_kernel,
        out_shape=(shape(1, 2, rows, cols),) * 2 + (shape(2, blocks, rows, LANES), shape(4, n + 1, 8, cols)),
        in_specs=[SMEM] + [VMEM] * 7,
        out_specs=(ANY, ANY, VMEM, VMEM),
        scratch_shapes=[vm(blocks, FINAL, LANES), vm(2, rows, cols), dma(1 + blocks)],
        compiler_params=PARAMS,
        cost_estimate=pl.CostEstimate(flops=10**6, bytes_accessed=2**21, transcendentals=0),
        name="ready",
    )(where, got, c_values, lo, hi, viscosity, *handed)
    advanced = pl.pallas_call(
        final_kernel,
        out_shape=shape(1, 2, rows, cols),
        in_specs=[SMEM] + [VMEM] * 6,
        out_specs=ANY,
        scratch_shapes=[
            vm(2, blocks, FINAL, LANES), vm(2, blocks, FINAL, LANES),
            vm(2, n, 8, cols), vm(2, n, 8, cols), dma(blocks),
        ],
        compiler_params=PARAMS,
        name="final",
    )(where, mine, above, below, lo, hi, cf)
    return corrected, advanced, defect


def solution(mesh):
    return jax.shard_map(
        shards,
        mesh=mesh,
        in_specs=(P("tm", None, "space", None), P("space", None)),
        out_specs=(P("tm", None, "space", None),) * 3,
        check_vma=False,
    )
```

```python
import functools

import jax
import jax.numpy as jnp
from jax import lax
from jax.experimental import pallas as pl
from jax.experimental.pallas import tpu as pltpu
from jax.sharding import PartitionSpec as P

STEPS = 8
GROUP = 8
STRIP = 16
HALO = 16
EDGE = 32
WINDOW = STRIP + 2 * HALO
INNER = 8
TIGHT = STRIP + 2 * INNER
FINAL = 96
LANES = 128
SPLIT = 4
advect_scale = 0.1
coarse_size = 1.0
COARSE = 0.5 * advect_scale * coarse_size
FINE = COARSE / STEPS
f32 = jnp.float32


def shift_up(plane):
    return pltpu.roll(plane, 1, 0)


def shift_down(plane):
    return pltpu.roll(plane, plane.shape[0] - 1, 0)


def left_of(x):
    return pltpu.roll(x, 1, 1)


def right_of(x):
    return pltpu.roll(x, x.shape[1] - 1, 1)


def make_coefs(planes, size, coef):
    cx, cyp, cym, dd = coef
    n = len(planes)
    faces = []
    for i in range(n):
        below = planes[i + 1] if i + 1 < n else shift_down(planes[0])
        faces.append((0.5 * size) * (planes[i] + below))
    first = shift_up(faces[n - 1])
    cx[0] = first
    for i in range(n):
        cx[i + 1] = faces[i]
        nyp = (0.5 * size) * (planes[i] + right_of(planes[i]))
        nym = left_of(nyp)
        cyp[i] = nyp
        cym[i] = nym
        nxm = faces[i - 1] if i > 0 else first
        dd[i] = 1.0 - ((faces[i] + nxm) + (nyp + nym))


def euler(src, coef, n, emit):
    cx, cyp, cym, dd = coef
    above = [shift_up(src[c, n - 1]) for c in range(2)]
    here = [src[c, 0] for c in range(2)]
    first = here
    for i in range(n):
        if i + 1 < n:
            below = [src[c, i + 1] for c in range(2)]
        else:
            below = [shift_down(first[c]) for c in range(2)]
        wxp = cx[i + 1] - here[0]
        wxm = cx[i] + here[0]
        wyp = cyp[i] - here[1]
        wym = cym[i] + here[1]
        d = dd[i]
        res = []
        for c in range(2):
            f = here[c]
            res.append(
                (d * f + (wxp * below[c] + wxm * above[c]))
                + (wyp * right_of(f) + wym * left_of(f))
            )
        emit(i, res)
        above, here = here, below


def heun(src, mid, dst, coef, n, extra=None):
    def to_mid(i, res):
        for c in range(2):
            mid[c, i] = res[c]

    euler(src, coef, n, to_mid)

    def to_dst(i, res):
        for c in range(2):
            out = 0.5 * (src[c, i] + res[c])
            if extra is not None:
                out = out + extra(c, i)
            dst[c, i] = out

    euler(mid, coef, n, to_dst)


def plane(nat, i, n, first=0):
    return jnp.concatenate(
        [nat[b, pl.ds(first + i, 8, stride=n), :] for b in range(nat.shape[0])], axis=1
    )


def put_plane(nat, i, n, value):
    for b in range(nat.shape[0]):
        nat[b, pl.ds(i, 8, stride=n), :] = value[:, b * LANES : (b + 1) * LANES]


def load_planes(nat, n, first=0):
    return [plane(nat, i, n, first) for i in range(n)]


def fill(nat, at, ref, start, count):
    for b in range(nat.shape[0]):
        nat[b, at : at + count, :] = ref[start : start + count, b * LANES : (b + 1) * LANES]


def copies(pairs, sem):
    started = [pltpu.make_async_copy(a, b, sem.at[i]) for i, (a, b) in enumerate(pairs)]
    for copy in started:
        copy.start()
    return started


def edges_kernel(c_ref, n_ref, top_ref, bottom_ref, held, sem):
    rows = n_ref.shape[0]
    pairs, later = [], []
    for k, (out, start) in enumerate(((top_ref, 0), (bottom_ref, rows - EDGE))):
        pairs.append((c_ref.at[0, :, pl.ds(start, EDGE), :], held.at[k, pl.ds(0, 2)]))
        pairs.append((n_ref.at[pl.ds(start, EDGE), :], held.at[k, 2]))
        later += [(held.at[k, pl.ds(0, 2)], out.at[pl.ds(0, 2)]), (held.at[k, 2], out.at[2])]
    started = copies(pairs, sem)
    sent = []
    for i, copy in enumerate(started):
        copy.wait()
        sent += copies([later[i]], sem.at[pl.ds(4 + i, 1)])
    for copy in sent:
        copy.wait()


def load_kernel(c_ref, n_ref, out_ref, sem):
    pairs = [(c_ref.at[0], out_ref.at[pl.ds(0, 2)]), (n_ref, out_ref.at[2])]
    for copy in copies(pairs, sem):
        copy.wait()


def cut(b):
    return pl.ds(b * LANES, LANES)


def forward_kernel(where_ref, own_ref, lo_ref, hi_ref,
                   fwd_ref, nwin_ref, own_tau, far0, far1, far2, far3,
                   nat, fnat, w, mid, tau, cf, cc, sem):
    n = 16
    blocks = nat.shape[1]
    rows = own_ref.shape[1]
    for c in (2, 0, 1):
        fill(nat.at[c], 0, lo_ref.at[c], 0, EDGE)
        fill(nat.at[c], EDGE, own_ref.at[c], 0, rows)
        fill(nat.at[c], EDGE + rows, hi_ref.at[c], 0, EDGE)
    position = where_ref[0]
    vnat = nat.at[2]
    start = pl.multiple_of(lax.rem(position, SPLIT) * STRIP + HALO, 8)
    nwin_ref[...] = nat[2, :, pl.ds(start, WINDOW), :]
    visc = load_planes(vnat, n)
    coef_c = [cc.at[i] for i in range(4)]
    coef_f = [cf.at[i] for i in range(4)]
    make_coefs(visc, coarse_size, coef_c)
    for i in range(n + 1):
        cf[0, i] = cc[0, i] * (1.0 / STEPS)
    for i in range(n):
        cf[1, i] = cc[1, i] * (1.0 / STEPS)
        cf[2, i] = cc[2, i] * (1.0 / STEPS)
        cf[3, i] = cc[3, i] * (1.0 / STEPS) + (1.0 - 1.0 / STEPS)
    for c in range(2):
        for i in range(n):
            w[c, i] = COARSE * plane(nat.at[c], i, n)
    heun(w, mid, tau, coef_c, n)
    for c in range(2):
        for i in range(n):
            w[c, i] = w[c, i] * (FINE / COARSE)

    def step(_, carry):
        heun(w, mid, w, coef_f, n)
        return carry

    lax.fori_loop(0, STEPS, step, 0)
    keep = jnp.where(position == 0, 0.0, 1.0).astype(f32)
    for c in range(2):
        for i in range(n):
            end = w[c, i] * (COARSE / FINE)
            put_plane(nat.at[c], i, n, end - keep * tau[c, i])
            put_plane(fnat.at[c], i, n, end * (1.0 / COARSE))
    pairs = []
    for b in range(blocks):
        both = pl.ds(0, 2)
        pairs.append((fnat.at[both, b, pl.ds(EDGE, rows), :], fwd_ref.at[both, :, cut(b)]))
    started = copies(pairs, sem)
    for k in range(SPLIT):
        first = k * STRIP + (EDGE - HALO)
        own_tau[k] = nat[0:2, :, first : first + WINDOW, :]
    for k, ref in enumerate((far0, far1, far2, far3)):
        first = lax.rem(position + k, SPLIT) * STRIP + (EDGE - INNER)
        ref[...] = nat[0:2, :, pl.ds(pl.multiple_of(first, 8), TIGHT), :]
    for copy in started:
        copy.wait()


def prep_kernel(nwin_ref, wide_ref, tight_ref):
    wide = [wide_ref.at[i] for i in range(4)]
    tight = [tight_ref.at[i] for i in range(4)]
    make_coefs(load_planes(nwin_ref, WINDOW // 8), coarse_size, wide)
    make_coefs(load_planes(nwin_ref, TIGHT // 8, HALO - INNER), coarse_size, tight)


def chain_kernel(stage, stages, carried, *refs):
    refs = list(refs)
    where_ref, wide_ref, tight_ref = refs[:3]
    nat, w, mid, nat_t, w_t, mid_t = refs[-6:]
    if stage + 1 < stages:
        last_ref = refs.pop(-7)
    corr_ref = refs[-7]
    n, n_t = WINDOW // 8, TIGHT // 8
    position = where_ref[0]
    planes = GROUP // SPLIT
    rest = refs[3 + carried :]
    if stage == 0:
        near_ref, far_ref = rest[0], refs[-8]
        for k in range(SPLIT):
            source = lax.rem(position + SPLIT - k, SPLIT)
            far_ref[source] = rest[1 + k][...]
    else:
        near_ref, far_ref, own, pair, other, corr_in = rest[:6]
    active = position // SPLIT == stage * planes

    @pl.when(active)
    def _():
        wide = [wide_ref.at[i] for i in range(4)]
        tight = [tight_ref.at[i] for i in range(4)]

        def keep(out):
            for c in range(2):
                for i in range(n):
                    put_plane(nat.at[c], i, n, w[c, i])
                out[c] = nat[c, :, HALO : HALO + STRIP, :]

        def one(t, out):
            heun(w, mid, w, wide, n, lambda c, i: plane(near_ref.at[t, c], i, n))
            keep(out)

        def one_tight(t, out):
            heun(w_t, mid_t, w_t, tight, n_t, lambda c, i: plane(far_ref.at[t - SPLIT, c], i, n_t))
            for c in range(2):
                for i in range(n_t):
                    put_plane(nat_t.at[c], i, n_t, w_t[c, i])
                out[c] = nat_t[c, :, INNER : INNER + STRIP, :]

        if stage == 0:
            for c in range(2):
                corr_ref[0, c] = jnp.zeros_like(corr_ref[0, c])
                for i in range(n):
                    w[c, i] = plane(near_ref.at[0, c], i, n)
            keep(corr_ref.at[1])
        else:
            even = lax.rem(position, 2) == 0
            for choice, refs_in_order in ((even, (other, own, pair)), (jnp.logical_not(even), (pair, own, other))):

                @pl.when(choice)
                def _():
                    for c in range(2):
                        for k, ref in enumerate(refs_in_order):
                            nat[c, :, k * STRIP : (k + 1) * STRIP, :] = ref[c]

            for c in range(2):
                corr_ref[0, c] = own[c]
                for i in range(n):
                    w[c, i] = plane(nat.at[c], i, n)
            one(0, corr_ref.at[1])

        def step(t, carry):
            one(t, corr_ref.at[t + 1])
            return carry

        def step_tight(t, carry):
            one_tight(t, corr_ref.at[t + 1])
            return carry

        lax.fori_loop(1, SPLIT, step, 0)
        for c in range(2):
            for i in range(n_t):
                w_t[c, i] = plane(nat.at[c], i, n_t, HALO - INNER)
        lax.fori_loop(SPLIT, GROUP - 1, step_tight, 0)
        if stage + 1 < stages:
            one_tight(GROUP - 1, last_ref)

    if stage > 0:

        @pl.when(jnp.logical_not(active))
        def _():
            corr_ref[...] = corr_in[...]


def ready_kernel(where_ref, got_ref, c_ref, clo_ref, chi_ref, n_ref, handed_ref, handed2_ref,
                 corr_ref, defect_ref, own_ref, cf_ref,
                 vnat, dbuf, sem):
    n = FINAL // 8
    rows = n_ref.shape[0]
    blocks = vnat.shape[0]
    position = where_ref[0]

    @pl.when(position == 0)
    def _():
        for c in range(2):
            dbuf[c] = jnp.zeros_like(dbuf[c])
            fill(own_ref.at[c], 0, c_ref.at[0, c], 0, rows)

    @pl.when(position != 0)
    def _():
        back = 1.0 / COARSE
        for c in range(2):
            dbuf[c] = (handed_ref[c] + handed2_ref[c]) - c_ref[0, c]
            for q in range(SPLIT):
                own_ref[c, :, q * STRIP : (q + 1) * STRIP, :] = back * got_ref[q, c]

    both = pl.ds(0, 2)
    pairs = [(dbuf, defect_ref.at[0])]
    for b in range(blocks):
        pairs.append((own_ref.at[both, b], corr_ref.at[0, both, :, cut(b)]))
    started = copies(pairs, sem)
    fill(vnat, 0, clo_ref.at[2], EDGE - HALO, HALO)
    fill(vnat, HALO, n_ref, 0, rows)
    fill(vnat, HALO + rows, chi_ref.at[2], 0, HALO)
    make_coefs(load_planes(vnat, n), coarse_size / STEPS, [cf_ref.at[i] for i in range(4)])
    for copy in started:
        copy.wait()


def final_kernel(where_ref, own_ref, lo_ref, hi_ref, clo_ref, chi_ref, cf_ref,
                 adv_ref,
                 nat, anat, w, mid, sem):
    n = FINAL // 8
    rows = own_ref.shape[2]
    blocks = nat.shape[1]
    position = where_ref[0]
    coef = [cf_ref.at[i] for i in range(4)]

    @pl.when(position == 0)
    def _():
        for c in range(2):
            fill(nat.at[c], 0, clo_ref.at[c], EDGE - HALO, HALO)
            fill(nat.at[c], HALO + rows, chi_ref.at[c], 0, HALO)

    @pl.when(position != 0)
    def _():
        back = 1.0 / COARSE
        for c in range(2):
            nat[c, :, 0:HALO, :] = back * lo_ref[c]
            nat[c, :, HALO + rows :, :] = back * hi_ref[c]

    both = pl.ds(0, 2)
    mine = pl.ds(HALO, rows)
    for c in range(2):
        nat[c, :, HALO : HALO + rows, :] = own_ref[c]
        for i in range(n):
            w[c, i] = FINE * plane(nat.at[c], i, n)

    def step(_, carry):
        heun(w, mid, w, coef, n)
        return carry

    lax.fori_loop(0, STEPS, step, 0)
    started = []
    for b in range(blocks):
        for c in range(2):
            for i in range(n):
                part = w[c, i, :, b * LANES : (b + 1) * LANES]
                anat[c, b, pl.ds(i, 8, stride=n), :] = part * (1.0 / FINE)
        pair = (anat.at[both, b, mine, :], adv_ref.at[0, both, :, cut(b)])
        started += copies([pair], sem.at[pl.ds(b, 1)])
    for copy in started:
        copy.wait()


VMEM = pl.BlockSpec(memory_space=pltpu.VMEM)
SMEM = pl.BlockSpec(memory_space=pltpu.SMEM)
ANY = pl.BlockSpec(memory_space=pl.ANY)
HBM = pl.BlockSpec(memory_space=pltpu.HBM)
FULL = pltpu.CompilerParams(vmem_limit_bytes=63 * 1024 * 1024)
PARAMS = pltpu.CompilerParams(vmem_limit_bytes=48 * 1024 * 1024)


def shards(c_values, viscosity):
    _, _, rows, cols = c_values.shape
    blocks = cols // LANES
    ring = lax.axis_size("space")
    intervals = lax.axis_size("tm")
    stages = intervals // GROUP
    up = [(i, (i + 1) % ring) for i in range(ring)]
    down = [(b, a) for a, b in up]
    where = lax.axis_index("tm").reshape(1).astype(jnp.int32)
    shape = lambda *s: jax.ShapeDtypeStruct(s, f32)
    vm = lambda *s: pltpu.VMEM(s, f32)
    dma = lambda k: pltpu.SemaphoreType.DMA((k,))

    top, bottom = pl.pallas_call(
        edges_kernel,
        out_shape=(shape(3, EDGE, cols),) * 2,
        in_specs=[HBM] * 2,
        out_specs=(ANY,) * 2,
        scratch_shapes=[vm(2, 3, EDGE, cols), dma(8)],
        compiler_params=FULL,
        name="edges",
    )(c_values, viscosity)
    own = pl.pallas_call(
        load_kernel,
        out_shape=shape(3, rows, cols),
        in_specs=[ANY] * 2,
        out_specs=ANY,
        scratch_shapes=[dma(2)],
        compiler_params=PARAMS,
        cost_estimate=pl.CostEstimate(flops=0, bytes_accessed=6 * rows * cols * 4, transcendentals=0),
        name="load",
    )(c_values, viscosity)
    lo = lax.ppermute(bottom, "space", up)
    hi = lax.ppermute(top, "space", down)

    n = 16
    window = shape(SPLIT, 2, blocks, WINDOW, LANES)
    inner = shape(2, blocks, TIGHT, LANES)
    forward, nwin, *sent = pl.pallas_call(
        forward_kernel,
        out_shape=(shape(2, rows, cols), shape(blocks, WINDOW, LANES)) + (window,) + (inner,) * SPLIT,
        in_specs=[SMEM, VMEM, VMEM, VMEM],
        out_specs=(HBM,) + (VMEM,) * (2 + SPLIT),
        scratch_shapes=[
            vm(3, blocks, 128, LANES), vm(2, blocks, 128, LANES),
            vm(2, n, 8, cols), vm(2, n, 8, cols), vm(2, n, 8, cols),
            vm(4, n + 1, 8, cols), vm(4, n + 1, 8, cols), dma(blocks),
        ],
        compiler_params=PARAMS,
        name="forward",
    )(where, own, lo, hi)

    n, n_t = WINDOW // 8, TIGHT // 8
    coefs = pl.pallas_call(
        prep_kernel,
        out_shape=(shape(4, n + 1, 8, cols), shape(4, n_t + 1, 8, cols)),
        in_specs=[VMEM],
        out_specs=(VMEM, VMEM),
        compiler_params=PARAMS,
        name="prep",
    )(nwin)

    planes = range(0, intervals, SPLIT)
    gathered = [sent[0]]
    four = [[p + q for q in range(SPLIT)] for p in planes]
    near = lax.all_to_all(sent[0], "tm", 0, 0, axis_index_groups=four)
    gathered = [near]
    for k in range(SPLIT):
        pairs = []
        for p in range(0, intervals, GROUP):
            for q in range(SPLIT):
                a, b = p + SPLIT + q, p + (q + k) % SPLIT
                pairs += [(a, b), (b, a)]
        gathered.append(lax.ppermute(sent[1 + k], "tm", pairs))
    groups = [[g * GROUP + j for j in range(GROUP)] for g in range(stages)]

    strips = ring * SPLIT
    pieces, handed = [], []
    for stage in range(stages):
        carries = stage in (0, stages - 2)
        extra = ([forward] if carries else []) + (handed if stage >= stages - 2 else [])
        operands = [where, *coefs] + extra + (gathered if stage == 0 else [*taus, *pieces, corr])
        specs = [SMEM, VMEM, VMEM] + [HBM] * len(extra) + [VMEM] * (len(operands) - 3 - len(extra))
        shapes = [shape(2, rows, cols) if carries else shape(8, LANES)]
        if stage == 0:
            shapes += [shape(SPLIT, 2, blocks, TIGHT, LANES)]
        shapes += [shape(GROUP, 2, blocks, STRIP, LANES)]
        shapes += [shape(2, blocks, STRIP, LANES)] if stage + 1 < stages else []
        aliases = {len(operands) - 1: 1} if stage > 0 else {}
        if carries:
            aliases[3] = 0
        done = pl.pallas_call(
            functools.partial(chain_kernel, stage, stages, len(extra)),
            out_shape=tuple(shapes),
            in_specs=specs,
            out_specs=(HBM,) + (VMEM,) * (len(shapes) - 1),
            scratch_shapes=[
                vm(2, blocks, WINDOW, LANES), vm(2, n, 8, cols), vm(2, n, 8, cols),
                vm(2, blocks, TIGHT, LANES), vm(2, n_t, 8, cols), vm(2, n_t, 8, cols),
            ],
            input_output_aliases=aliases,
            compiler_params=PARAMS,
            name="chain%d" % stage,
        )(*operands)
        if stage == 0:
            taus = [near, done[1]]
        corr, last = done[-2:] if stage + 1 < stages else (done[-1], None)
        if carries:
            forward = done[0]
            chain = [g * GROUP + q for g in range(2) for q in range(SPLIT)]
            pairs = [(i, i + 1) for i in range(intervals - 1) if (i in chain or i + 1 in chain) == (stage > 0)]
            handed = handed + [lax.ppermute(forward, "tm", pairs)]
        if stage + 1 < stages:
            pieces = []
            moves = (lambda q: q, lambda q: q + 1 - 2 * (q % 2), lambda q: (q - 1 + 2 * (q % 2)) % strips)
            for move in moves:
                pairs = []
                for strip in range(strips):
                    to = move(strip)
                    source = stage * GROUP + strip % SPLIT
                    target = (stage + 1) * GROUP + to % SPLIT
                    pairs.append((source * ring + strip // SPLIT, target * ring + to // SPLIT))
                pieces.append(lax.ppermute(last, ("tm", "space"), pairs))

    got = lax.all_to_all(corr, "tm", 0, 0, axis_index_groups=groups)
    above = lax.ppermute(got[SPLIT - 1], "space", up)
    below = lax.ppermute(got[0], "space", down)

    n = FINAL // 8
    corrected, defect, mine, cf = pl.pallas_call(
        ready_kernel,
        out_shape=(shape(1, 2, rows, cols),) * 2 + (shape(2, blocks, rows, LANES), shape(4, n + 1, 8, cols)),
        in_specs=[SMEM] + [VMEM] * 7,
        out_specs=(ANY, ANY, VMEM, VMEM),
        scratch_shapes=[vm(blocks, FINAL, LANES), vm(2, rows, cols), dma(1 + blocks)],
        compiler_params=PARAMS,
        cost_estimate=pl.CostEstimate(flops=10**6, bytes_accessed=2**21, transcendentals=0),
        name="ready",
    )(where, got, c_values, lo, hi, viscosity, *handed)
    advanced = pl.pallas_call(
        final_kernel,
        out_shape=shape(1, 2, rows, cols),
        in_specs=[SMEM] + [VMEM] * 6,
        out_specs=ANY,
        scratch_shapes=[
            vm(2, blocks, FINAL, LANES), vm(2, blocks, FINAL, LANES),
            vm(2, n, 8, cols), vm(2, n, 8, cols), dma(blocks),
        ],
        compiler_params=PARAMS,
        name="final",
    )(where, mine, above, below, lo, hi, cf)
    return corrected, advanced, defect


def solution(mesh):
    return jax.shard_map(
        shards,
        mesh=mesh,
        in_specs=(P("tm", None, "space", None), P("space", None)),
        out_specs=(P("tm", None, "space", None),) * 3,
        check_vma=False,
    )
```

```python
import functools

import jax
import jax.numpy as jnp
from jax import lax
from jax.experimental import pallas as pl
from jax.experimental.pallas import tpu as pltpu
from jax.sharding import PartitionSpec as P

STEPS = 8
GROUP = 8
STRIP = 16
HALO = 16
EDGE = 32
WINDOW = STRIP + 2 * HALO
INNER = 8
TIGHT = STRIP + 2 * INNER
FINAL = 96
LANES = 128
SPLIT = 4
advect_scale = 0.1
coarse_size = 1.0
COARSE = 0.5 * advect_scale * coarse_size
FINE = COARSE / STEPS
f32 = jnp.float32


def shift_up(plane):
    return pltpu.roll(plane, 1, 0)


def shift_down(plane):
    return pltpu.roll(plane, plane.shape[0] - 1, 0)


def left_of(x):
    return pltpu.roll(x, 1, 1)


def right_of(x):
    return pltpu.roll(x, x.shape[1] - 1, 1)


def make_coefs(planes, size, coef):
    cx, cyp, cym, dd = coef
    n = len(planes)
    faces = []
    for i in range(n):
        below = planes[i + 1] if i + 1 < n else shift_down(planes[0])
        faces.append((0.5 * size) * (planes[i] + below))
    first = shift_up(faces[n - 1])
    cx[0] = first
    for i in range(n):
        cx[i + 1] = faces[i]
        nyp = (0.5 * size) * (planes[i] + right_of(planes[i]))
        nym = left_of(nyp)
        cyp[i] = nyp
        cym[i] = nym
        nxm = faces[i - 1] if i > 0 else first
        dd[i] = 1.0 - ((faces[i] + nxm) + (nyp + nym))


def euler(src, coef, n, emit):
    cx, cyp, cym, dd = coef
    above = [shift_up(src[c, n - 1]) for c in range(2)]
    here = [src[c, 0] for c in range(2)]
    first = here
    for i in range(n):
        if i + 1 < n:
            below = [src[c, i + 1] for c in range(2)]
        else:
            below = [shift_down(first[c]) for c in range(2)]
        wxp = cx[i + 1] - here[0]
        wxm = cx[i] + here[0]
        wyp = cyp[i] - here[1]
        wym = cym[i] + here[1]
        d = dd[i]
        res = []
        for c in range(2):
            f = here[c]
            res.append(
                (d * f + (wxp * below[c] + wxm * above[c]))
                + (wyp * right_of(f) + wym * left_of(f))
            )
        emit(i, res)
        above, here = here, below


def heun(src, mid, dst, coef, n, extra=None):
    def to_mid(i, res):
        for c in range(2):
            mid[c, i] = res[c]

    euler(src, coef, n, to_mid)

    def to_dst(i, res):
        for c in range(2):
            out = 0.5 * (src[c, i] + res[c])
            if extra is not None:
                out = out + extra(c, i)
            dst[c, i] = out

    euler(mid, coef, n, to_dst)


def plane(nat, i, n, first=0):
    return jnp.concatenate(
        [nat[b, pl.ds(first + i, 8, stride=n), :] for b in range(nat.shape[0])], axis=1
    )


def put_plane(nat, i, n, value):
    for b in range(nat.shape[0]):
        nat[b, pl.ds(i, 8, stride=n), :] = value[:, b * LANES : (b + 1) * LANES]


def load_planes(nat, n, first=0):
    return [plane(nat, i, n, first) for i in range(n)]


def fill(nat, at, ref, start, count):
    for b in range(nat.shape[0]):
        nat[b, at : at + count, :] = ref[start : start + count, b * LANES : (b + 1) * LANES]


def copies(pairs, sem):
    started = [pltpu.make_async_copy(a, b, sem.at[i]) for i, (a, b) in enumerate(pairs)]
    for copy in started:
        copy.start()
    return started


def edges_kernel(c_ref, n_ref, top_ref, bottom_ref, held, sem):
    rows = n_ref.shape[0]
    pairs, later = [], []
    for k, (out, start) in enumerate(((top_ref, 0), (bottom_ref, rows - EDGE))):
        pairs.append((c_ref.at[0, :, pl.ds(start, EDGE), :], held.at[k, pl.ds(0, 2)]))
        pairs.append((n_ref.at[pl.ds(start, EDGE), :], held.at[k, 2]))
        later += [(held.at[k, pl.ds(0, 2)], out.at[pl.ds(0, 2)]), (held.at[k, 2], out.at[2])]
    started = copies(pairs, sem)
    sent = []
    for i, copy in enumerate(started):
        copy.wait()
        sent += copies([later[i]], sem.at[pl.ds(4 + i, 1)])
    for copy in sent:
        copy.wait()


def load_kernel(c_ref, n_ref, out_ref, sem):
    pairs = [(c_ref.at[0], out_ref.at[pl.ds(0, 2)]), (n_ref, out_ref.at[2])]
    for copy in copies(pairs, sem):
        copy.wait()


def cut(b):
    return pl.ds(b * LANES, LANES)


def forward_kernel(where_ref, own_ref, lo_ref, hi_ref,
                   fwd_ref, nwin_ref, own_tau, far0, far1, far2, far3,
                   nat, fnat, w, mid, tau, cf, cc, sem):
    n = 16
    blocks = nat.shape[1]
    rows = own_ref.shape[1]
    for c in (2, 0, 1):
        fill(nat.at[c], 0, lo_ref.at[c], 0, EDGE)
        fill(nat.at[c], EDGE, own_ref.at[c], 0, rows)
        fill(nat.at[c], EDGE + rows, hi_ref.at[c], 0, EDGE)
    position = where_ref[0]
    vnat = nat.at[2]
    start = pl.multiple_of(lax.rem(position, SPLIT) * STRIP + HALO, 8)
    nwin_ref[...] = nat[2, :, pl.ds(start, WINDOW), :]
    visc = load_planes(vnat, n)
    coef_c = [cc.at[i] for i in range(4)]
    coef_f = [cf.at[i] for i in range(4)]
    make_coefs(visc, coarse_size, coef_c)
    for i in range(n + 1):
        cf[0, i] = cc[0, i] * (1.0 / STEPS)
    for i in range(n):
        cf[1, i] = cc[1, i] * (1.0 / STEPS)
        cf[2, i] = cc[2, i] * (1.0 / STEPS)
        cf[3, i] = cc[3, i] * (1.0 / STEPS) + (1.0 - 1.0 / STEPS)
    for c in range(2):
        for i in range(n):
            w[c, i] = COARSE * plane(nat.at[c], i, n)
    heun(w, mid, tau, coef_c, n)
    for c in range(2):
        for i in range(n):
            w[c, i] = w[c, i] * (FINE / COARSE)

    def step(_, carry):
        heun(w, mid, w, coef_f, n)
        return carry

    lax.fori_loop(0, STEPS, step, 0, unroll=2)
    keep = jnp.where(position == 0, 0.0, 1.0).astype(f32)
    for c in range(2):
        for i in range(n):
            end = w[c, i] * (COARSE / FINE)
            put_plane(nat.at[c], i, n, end - keep * tau[c, i])
            put_plane(fnat.at[c], i, n, end * (1.0 / COARSE))
    pairs = []
    for b in range(blocks):
        both = pl.ds(0, 2)
        pairs.append((fnat.at[both, b, pl.ds(EDGE, rows), :], fwd_ref.at[both, :, cut(b)]))
    started = copies(pairs, sem)
    for k in range(SPLIT):
        first = k * STRIP + (EDGE - HALO)
        own_tau[k] = nat[0:2, :, first : first + WINDOW, :]
    for k, ref in enumerate((far0, far1, far2, far3)):
        first = lax.rem(position + k, SPLIT) * STRIP + (EDGE - INNER)
        ref[...] = nat[0:2, :, pl.ds(pl.multiple_of(first, 8), TIGHT), :]
    for copy in started:
        copy.wait()


def prep_kernel(nwin_ref, wide_ref, tight_ref):
    wide = [wide_ref.at[i] for i in range(4)]
    tight = [tight_ref.at[i] for i in range(4)]
    make_coefs(load_planes(nwin_ref, WINDOW // 8), coarse_size, wide)
    make_coefs(load_planes(nwin_ref, TIGHT // 8, HALO - INNER), coarse_size, tight)


def chain_kernel(stage, stages, carried, *refs):
    refs = list(refs)
    where_ref, wide_ref, tight_ref = refs[:3]
    nat, w, mid, nat_t, w_t, mid_t = refs[-6:]
    if stage + 1 < stages:
        last_ref = refs.pop(-7)
    corr_ref = refs[-7]
    n, n_t = WINDOW // 8, TIGHT // 8
    position = where_ref[0]
    planes = GROUP // SPLIT
    rest = refs[3 + carried :]
    if stage == 0:
        near_ref, far_ref = rest[0], refs[-8]
        for k in range(SPLIT):
            source = lax.rem(position + SPLIT - k, SPLIT)
            far_ref[source] = rest[1 + k][...]
    else:
        near_ref, far_ref, own, pair, other, corr_in = rest[:6]
    active = position // SPLIT == stage * planes

    @pl.when(active)
    def _():
        wide = [wide_ref.at[i] for i in range(4)]
        tight = [tight_ref.at[i] for i in range(4)]

        def keep(out):
            for c in range(2):
                for i in range(n):
                    put_plane(nat.at[c], i, n, w[c, i])
                out[c] = nat[c, :, HALO : HALO + STRIP, :]

        def one(t, out):
            heun(w, mid, w, wide, n, lambda c, i: plane(near_ref.at[t, c], i, n))
            keep(out)

        def one_tight(t, out):
            heun(w_t, mid_t, w_t, tight, n_t, lambda c, i: plane(far_ref.at[t - SPLIT, c], i, n_t))
            for c in range(2):
                for i in range(n_t):
                    put_plane(nat_t.at[c], i, n_t, w_t[c, i])
                out[c] = nat_t[c, :, INNER : INNER + STRIP, :]

        if stage == 0:
            for c in range(2):
                corr_ref[0, c] = jnp.zeros_like(corr_ref[0, c])
                for i in range(n):
                    w[c, i] = plane(near_ref.at[0, c], i, n)
            keep(corr_ref.at[1])
        else:
            even = lax.rem(position, 2) == 0
            for choice, refs_in_order in ((even, (other, own, pair)), (jnp.logical_not(even), (pair, own, other))):

                @pl.when(choice)
                def _():
                    for c in range(2):
                        for k, ref in enumerate(refs_in_order):
                            nat[c, :, k * STRIP : (k + 1) * STRIP, :] = ref[c]

            for c in range(2):
                corr_ref[0, c] = own[c]
                for i in range(n):
                    w[c, i] = plane(nat.at[c], i, n)
            one(0, corr_ref.at[1])

        def step(t, carry):
            one(t, corr_ref.at[t + 1])
            return carry

        def step_tight(t, carry):
            one_tight(t, corr_ref.at[t + 1])
            return carry

        lax.fori_loop(1, SPLIT, step, 0, unroll=True)
        for c in range(2):
            for i in range(n_t):
                w_t[c, i] = plane(nat.at[c], i, n_t, HALO - INNER)
        lax.fori_loop(SPLIT, GROUP - 1, step_tight, 0, unroll=True)
        if stage + 1 < stages:
            one_tight(GROUP - 1, last_ref)

    if stage > 0:

        @pl.when(jnp.logical_not(active))
        def _():
            corr_ref[...] = corr_in[...]


def ready_kernel(where_ref, got_ref, c_ref, clo_ref, chi_ref, n_ref, handed_ref, handed2_ref,
                 corr_ref, defect_ref, own_ref, cf_ref,
                 vnat, dbuf, sem):
    n = FINAL // 8
    rows = n_ref.shape[0]
    blocks = vnat.shape[0]
    position = where_ref[0]

    @pl.when(position == 0)
    def _():
        for c in range(2):
            dbuf[c] = jnp.zeros_like(dbuf[c])
            fill(own_ref.at[c], 0, c_ref.at[0, c], 0, rows)

    @pl.when(position != 0)
    def _():
        back = 1.0 / COARSE
        for c in range(2):
            dbuf[c] = (handed_ref[c] + handed2_ref[c]) - c_ref[0, c]
            for q in range(SPLIT):
                own_ref[c, :, q * STRIP : (q + 1) * STRIP, :] = back * got_ref[q, c]

    both = pl.ds(0, 2)
    pairs = [(dbuf, defect_ref.at[0])]
    for b in range(blocks):
        pairs.append((own_ref.at[both, b], corr_ref.at[0, both, :, cut(b)]))
    started = copies(pairs, sem)
    fill(vnat, 0, clo_ref.at[2], EDGE - HALO, HALO)
    fill(vnat, HALO, n_ref, 0, rows)
    fill(vnat, HALO + rows, chi_ref.at[2], 0, HALO)
    make_coefs(load_planes(vnat, n), coarse_size / STEPS, [cf_ref.at[i] for i in range(4)])
    for copy in started:
        copy.wait()


def final_kernel(where_ref, own_ref, lo_ref, hi_ref, clo_ref, chi_ref, cf_ref,
                 adv_ref,
                 nat, anat, w, mid, sem):
    n = FINAL // 8
    rows = own_ref.shape[2]
    blocks = nat.shape[1]
    position = where_ref[0]
    coef = [cf_ref.at[i] for i in range(4)]

    @pl.when(position == 0)
    def _():
        for c in range(2):
            fill(nat.at[c], 0, clo_ref.at[c], EDGE - HALO, HALO)
            fill(nat.at[c], HALO + rows, chi_ref.at[c], 0, HALO)

    @pl.when(position != 0)
    def _():
        back = 1.0 / COARSE
        for c in range(2):
            nat[c, :, 0:HALO, :] = back * lo_ref[c]
            nat[c, :, HALO + rows :, :] = back * hi_ref[c]

    both = pl.ds(0, 2)
    mine = pl.ds(HALO, rows)
    for c in range(2):
        nat[c, :, HALO : HALO + rows, :] = own_ref[c]
        for i in range(n):
            w[c, i] = FINE * plane(nat.at[c], i, n)

    def step(_, carry):
        heun(w, mid, w, coef, n)
        return carry

    lax.fori_loop(0, STEPS, step, 0, unroll=2)
    started = []
    for b in range(blocks):
        for c in range(2):
            for i in range(n):
                part = w[c, i, :, b * LANES : (b + 1) * LANES]
                anat[c, b, pl.ds(i, 8, stride=n), :] = part * (1.0 / FINE)
        pair = (anat.at[both, b, mine, :], adv_ref.at[0, both, :, cut(b)])
        started += copies([pair], sem.at[pl.ds(b, 1)])
    for copy in started:
        copy.wait()


VMEM = pl.BlockSpec(memory_space=pltpu.VMEM)
SMEM = pl.BlockSpec(memory_space=pltpu.SMEM)
ANY = pl.BlockSpec(memory_space=pl.ANY)
HBM = pl.BlockSpec(memory_space=pltpu.HBM)
FULL = pltpu.CompilerParams(vmem_limit_bytes=63 * 1024 * 1024)
PARAMS = pltpu.CompilerParams(vmem_limit_bytes=48 * 1024 * 1024)


def shards(c_values, viscosity):
    _, _, rows, cols = c_values.shape
    blocks = cols // LANES
    ring = lax.axis_size("space")
    intervals = lax.axis_size("tm")
    stages = intervals // GROUP
    up = [(i, (i + 1) % ring) for i in range(ring)]
    down = [(b, a) for a, b in up]
    where = lax.axis_index("tm").reshape(1).astype(jnp.int32)
    shape = lambda *s: jax.ShapeDtypeStruct(s, f32)
    vm = lambda *s: pltpu.VMEM(s, f32)
    dma = lambda k: pltpu.SemaphoreType.DMA((k,))

    top, bottom = pl.pallas_call(
        edges_kernel,
        out_shape=(shape(3, EDGE, cols),) * 2,
        in_specs=[HBM] * 2,
        out_specs=(ANY,) * 2,
        scratch_shapes=[vm(2, 3, EDGE, cols), dma(8)],
        compiler_params=FULL,
        name="edges",
    )(c_values, viscosity)
    own = pl.pallas_call(
        load_kernel,
        out_shape=shape(3, rows, cols),
        in_specs=[ANY] * 2,
        out_specs=ANY,
        scratch_shapes=[dma(2)],
        compiler_params=PARAMS,
        cost_estimate=pl.CostEstimate(flops=0, bytes_accessed=6 * rows * cols * 4, transcendentals=0),
        name="load",
    )(c_values, viscosity)
    lo = lax.ppermute(bottom, "space", up)
    hi = lax.ppermute(top, "space", down)

    n = 16
    window = shape(SPLIT, 2, blocks, WINDOW, LANES)
    inner = shape(2, blocks, TIGHT, LANES)
    forward, nwin, *sent = pl.pallas_call(
        forward_kernel,
        out_shape=(shape(2, rows, cols), shape(blocks, WINDOW, LANES)) + (window,) + (inner,) * SPLIT,
        in_specs=[SMEM, VMEM, VMEM, VMEM],
        out_specs=(HBM,) + (VMEM,) * (2 + SPLIT),
        scratch_shapes=[
            vm(3, blocks, 128, LANES), vm(2, blocks, 128, LANES),
            vm(2, n, 8, cols), vm(2, n, 8, cols), vm(2, n, 8, cols),
            vm(4, n + 1, 8, cols), vm(4, n + 1, 8, cols), dma(blocks),
        ],
        compiler_params=PARAMS,
        name="forward",
    )(where, own, lo, hi)

    n, n_t = WINDOW // 8, TIGHT // 8
    coefs = pl.pallas_call(
        prep_kernel,
        out_shape=(shape(4, n + 1, 8, cols), shape(4, n_t + 1, 8, cols)),
        in_specs=[VMEM],
        out_specs=(VMEM, VMEM),
        compiler_params=PARAMS,
        name="prep",
    )(nwin)

    planes = range(0, intervals, SPLIT)
    gathered = [sent[0]]
    four = [[p + q for q in range(SPLIT)] for p in planes]
    near = lax.all_to_all(sent[0], "tm", 0, 0, axis_index_groups=four)
    gathered = [near]
    for k in range(SPLIT):
        pairs = []
        for p in range(0, intervals, GROUP):
            for q in range(SPLIT):
                a, b = p + SPLIT + q, p + (q + k) % SPLIT
                pairs += [(a, b), (b, a)]
        gathered.append(lax.ppermute(sent[1 + k], "tm", pairs))
    groups = [[g * GROUP + j for j in range(GROUP)] for g in range(stages)]

    strips = ring * SPLIT
    pieces, handed = [], []
    for stage in range(stages):
        carries = stage in (1, stages - 2)
        extra = ([forward] if carries else []) + (handed if stage == stages - 1 else [])
        operands = [where, *coefs] + extra + (gathered if stage == 0 else [*taus, *pieces, corr])
        specs = [SMEM, VMEM, VMEM] + [HBM] * len(extra) + [VMEM] * (len(operands) - 3 - len(extra))
        shapes = [shape(2, rows, cols) if carries else shape(8, LANES)]
        if stage == 0:
            shapes += [shape(SPLIT, 2, blocks, TIGHT, LANES)]
        shapes += [shape(GROUP, 2, blocks, STRIP, LANES)]
        shapes += [shape(2, blocks, STRIP, LANES)] if stage + 1 < stages else []
        aliases = {len(operands) - 1: 1} if stage > 0 else {}
        if carries:
            aliases[3] = 0
        done = pl.pallas_call(
            functools.partial(chain_kernel, stage, stages, len(extra)),
            out_shape=tuple(shapes),
            in_specs=specs,
            out_specs=(HBM,) + (VMEM,) * (len(shapes) - 1),
            scratch_shapes=[
                vm(2, blocks, WINDOW, LANES), vm(2, n, 8, cols), vm(2, n, 8, cols),
                vm(2, blocks, TIGHT, LANES), vm(2, n_t, 8, cols), vm(2, n_t, 8, cols),
            ],
            input_output_aliases=aliases,
            compiler_params=PARAMS,
            name="chain%d" % stage,
        )(*operands)
        if stage == 0:
            taus = [near, done[1]]
        corr, last = done[-2:] if stage + 1 < stages else (done[-1], None)
        if carries:
            forward = done[0]
            chain = [g * GROUP + q for g in range(2) for q in range(SPLIT)]
            pairs = [(i, i + 1) for i in range(intervals - 1) if (i in chain or i + 1 in chain) == (stage == stages - 2)]
            handed = handed + [lax.ppermute(forward, "tm", pairs)]
        if stage + 1 < stages:
            pieces = []
            moves = (lambda q: q, lambda q: q + 1 - 2 * (q % 2), lambda q: (q - 1 + 2 * (q % 2)) % strips)
            for move in moves:
                pairs = []
                for strip in range(strips):
                    to = move(strip)
                    source = stage * GROUP + strip % SPLIT
                    target = (stage + 1) * GROUP + to % SPLIT
                    pairs.append((source * ring + strip // SPLIT, target * ring + to // SPLIT))
                pieces.append(lax.ppermute(last, ("tm", "space"), pairs))

    got = lax.all_to_all(corr, "tm", 0, 0, axis_index_groups=groups)
    above = lax.ppermute(got[SPLIT - 1], "space", up)
    below = lax.ppermute(got[0], "space", down)

    n = FINAL // 8
    corrected, defect, mine, cf = pl.pallas_call(
        ready_kernel,
        out_shape=(shape(1, 2, rows, cols),) * 2 + (shape(2, blocks, rows, LANES), shape(4, n + 1, 8, cols)),
        in_specs=[SMEM] + [VMEM] * 7,
        out_specs=(ANY, ANY, VMEM, VMEM),
        scratch_shapes=[vm(blocks, FINAL, LANES), vm(2, rows, cols), dma(1 + blocks)],
        compiler_params=PARAMS,
        cost_estimate=pl.CostEstimate(flops=10**6, bytes_accessed=2**21, transcendentals=0),
        name="ready",
    )(where, got, c_values, lo, hi, viscosity, *handed)
    advanced = pl.pallas_call(
        final_kernel,
        out_shape=shape(1, 2, rows, cols),
        in_specs=[SMEM] + [VMEM] * 6,
        out_specs=ANY,
        scratch_shapes=[
            vm(2, blocks, FINAL, LANES), vm(2, blocks, FINAL, LANES),
            vm(2, n, 8, cols), vm(2, n, 8, cols), dma(blocks),
        ],
        compiler_params=PARAMS,
        name="final",
    )(where, mine, above, below, lo, hi, cf)
    return corrected, advanced, defect


def solution(mesh):
    return jax.shard_map(
        shards,
        mesh=mesh,
        in_specs=(P("tm", None, "space", None), P("space", None)),
        out_specs=(P("tm", None, "space", None),) * 3,
        check_vma=False,
    )
```

```python
import functools

import jax
import jax.numpy as jnp
from jax import lax
from jax.experimental import pallas as pl
from jax.experimental.pallas import tpu as pltpu
from jax.sharding import PartitionSpec as P

STEPS = 8
GROUP = 8
STRIP = 16
HALO = 16
EDGE = 32
WINDOW = STRIP + 2 * HALO
INNER = 8
TIGHT = STRIP + 2 * INNER
FINAL = 96
LANES = 128
SPLIT = 4
FAR_ORDER = (2, 1, 3, 0)
advect_scale = 0.1
coarse_size = 1.0
COARSE = 0.5 * advect_scale * coarse_size
FINE = COARSE / STEPS
f32 = jnp.float32


def shift_up(plane):
    return pltpu.roll(plane, 1, 0)


def shift_down(plane):
    return pltpu.roll(plane, plane.shape[0] - 1, 0)


def left_of(x):
    return pltpu.roll(x, 1, 1)


def right_of(x):
    return pltpu.roll(x, x.shape[1] - 1, 1)


def make_coefs(planes, size, coef):
    cx, cyp, cym, dd = coef
    n = len(planes)
    faces = []
    for i in range(n):
        below = planes[i + 1] if i + 1 < n else shift_down(planes[0])
        faces.append((0.5 * size) * (planes[i] + below))
    first = shift_up(faces[n - 1])
    cx[0] = first
    for i in range(n):
        cx[i + 1] = faces[i]
        nyp = (0.5 * size) * (planes[i] + right_of(planes[i]))
        nym = left_of(nyp)
        cyp[i] = nyp
        cym[i] = nym
        nxm = faces[i - 1] if i > 0 else first
        dd[i] = 1.0 - ((faces[i] + nxm) + (nyp + nym))


def euler(src, coef, n, emit):
    cx, cyp, cym, dd = coef
    above = [shift_up(src[c, n - 1]) for c in range(2)]
    here = [src[c, 0] for c in range(2)]
    first = here
    for i in range(n):
        if i + 1 < n:
            below = [src[c, i + 1] for c in range(2)]
        else:
            below = [shift_down(first[c]) for c in range(2)]
        wxp = cx[i + 1] - here[0]
        wxm = cx[i] + here[0]
        wyp = cyp[i] - here[1]
        wym = cym[i] + here[1]
        d = dd[i]
        res = []
        for c in range(2):
            f = here[c]
            res.append(
                (d * f + (wxp * below[c] + wxm * above[c]))
                + (wyp * right_of(f) + wym * left_of(f))
            )
        emit(i, res)
        above, here = here, below


def heun(src, mid, dst, coef, n, extra=None):
    def to_mid(i, res):
        for c in range(2):
            mid[c, i] = res[c]

    euler(src, coef, n, to_mid)

    def to_dst(i, res):
        for c in range(2):
            out = 0.5 * (src[c, i] + res[c])
            if extra is not None:
                out = out + extra(c, i)
            dst[c, i] = out

    euler(mid, coef, n, to_dst)


def plane(nat, i, n, first=0):
    return jnp.concatenate(
        [nat[b, pl.ds(first + i, 8, stride=n), :] for b in range(nat.shape[0])], axis=1
    )


def put_plane(nat, i, n, value):
    for b in range(nat.shape[0]):
        nat[b, pl.ds(i, 8, stride=n), :] = value[:, b * LANES : (b + 1) * LANES]


def load_planes(nat, n, first=0):
    return [plane(nat, i, n, first) for i in range(n)]


def fill(nat, at, ref, start, count):
    for b in range(nat.shape[0]):
        nat[b, at : at + count, :] = ref[start : start + count, b * LANES : (b + 1) * LANES]


def copies(pairs, sem):
    started = [pltpu.make_async_copy(a, b, sem.at[i]) for i, (a, b) in enumerate(pairs)]
    for copy in started:
        copy.start()
    return started


def edges_kernel(c_ref, n_ref, top_ref, bottom_ref, held, sem):
    rows = n_ref.shape[0]
    pairs, later = [], []
    for k, (out, start) in enumerate(((top_ref, 0), (bottom_ref, rows - EDGE))):
        pairs.append((c_ref.at[0, :, pl.ds(start, EDGE), :], held.at[k, pl.ds(0, 2)]))
        pairs.append((n_ref.at[pl.ds(start, EDGE), :], held.at[k, 2]))
        later += [(held.at[k, pl.ds(0, 2)], out.at[pl.ds(0, 2)]), (held.at[k, 2], out.at[2])]
    started = copies(pairs, sem)
    sent = []
    for i, copy in enumerate(started):
        copy.wait()
        sent += copies([later[i]], sem.at[pl.ds(4 + i, 1)])
    for copy in sent:
        copy.wait()


def load_kernel(c_ref, n_ref, out_ref, sem):
    pairs = [(c_ref.at[0], out_ref.at[pl.ds(0, 2)]), (n_ref, out_ref.at[2])]
    for copy in copies(pairs, sem):
        copy.wait()


def cut(b):
    return pl.ds(b * LANES, LANES)


def forward_kernel(where_ref, own_ref, lo_ref, hi_ref,
                   fwd_ref, nwin_ref, own_tau, far0, far1, far2, far3,
                   nat, fnat, w, mid, tau, cf, cc, sem):
    n = 16
    blocks = nat.shape[1]
    rows = own_ref.shape[1]
    for c in (2, 0, 1):
        fill(nat.at[c], 0, lo_ref.at[c], 0, EDGE)
        fill(nat.at[c], EDGE, own_ref.at[c], 0, rows)
        fill(nat.at[c], EDGE + rows, hi_ref.at[c], 0, EDGE)
    position = where_ref[0]
    vnat = nat.at[2]
    start = pl.multiple_of(lax.rem(position, SPLIT) * STRIP + HALO, 8)
    nwin_ref[...] = nat[2, :, pl.ds(start, WINDOW), :]
    visc = load_planes(vnat, n)
    coef_c = [cc.at[i] for i in range(4)]
    coef_f = [cf.at[i] for i in range(4)]
    make_coefs(visc, coarse_size, coef_c)
    for i in range(n + 1):
        cf[0, i] = cc[0, i] * (1.0 / STEPS)
    for i in range(n):
        cf[1, i] = cc[1, i] * (1.0 / STEPS)
        cf[2, i] = cc[2, i] * (1.0 / STEPS)
        cf[3, i] = cc[3, i] * (1.0 / STEPS) + (1.0 - 1.0 / STEPS)
    for c in range(2):
        for i in range(n):
            w[c, i] = COARSE * plane(nat.at[c], i, n)
    heun(w, mid, tau, coef_c, n)
    for c in range(2):
        for i in range(n):
            w[c, i] = w[c, i] * (FINE / COARSE)

    def step(_, carry):
        heun(w, mid, w, coef_f, n)
        return carry

    lax.fori_loop(0, STEPS, step, 0, unroll=2)
    keep = jnp.where(position == 0, 0.0, 1.0).astype(f32)
    for c in range(2):
        for i in range(n):
            end = w[c, i] * (COARSE / FINE)
            put_plane(nat.at[c], i, n, end - keep * tau[c, i])
            put_plane(fnat.at[c], i, n, end * (1.0 / COARSE))
    pairs = []
    for b in range(blocks):
        both = pl.ds(0, 2)
        pairs.append((fnat.at[both, b, pl.ds(EDGE, rows), :], fwd_ref.at[both, :, cut(b)]))
    started = copies(pairs, sem)
    for k in range(SPLIT):
        first = k * STRIP + (EDGE - HALO)
        own_tau[k] = nat[0:2, :, first : first + WINDOW, :]
    for k, ref in enumerate((far0, far1, far2, far3)):
        first = lax.rem(position + k, SPLIT) * STRIP + (EDGE - INNER)
        ref[...] = nat[0:2, :, pl.ds(pl.multiple_of(first, 8), TIGHT), :]
    for copy in started:
        copy.wait()


def prep_kernel(nwin_ref, wide_ref, tight_ref):
    wide = [wide_ref.at[i] for i in range(4)]
    tight = [tight_ref.at[i] for i in range(4)]
    make_coefs(load_planes(nwin_ref, WINDOW // 8), coarse_size, wide)
    make_coefs(load_planes(nwin_ref, TIGHT // 8, HALO - INNER), coarse_size, tight)


def chain_kernel(stage, stages, carried, *refs):
    refs = list(refs)
    where_ref, wide_ref, tight_ref = refs[:3]
    nat, w, mid, nat_t, w_t, mid_t = refs[-6:]
    if stage + 1 < stages:
        last_ref = refs.pop(-7)
    corr_ref = refs[-7]
    n, n_t = WINDOW // 8, TIGHT // 8
    position = where_ref[0]
    planes = GROUP // SPLIT
    rest = refs[3 + carried :]
    if stage == 0:
        near_ref, far_ref = rest[0], refs[-8]
        for i, k in enumerate(FAR_ORDER):
            source = lax.rem(position + SPLIT - k, SPLIT)
            far_ref[source] = rest[1 + i][...]
    else:
        near_ref, far_ref, own, pair, other, corr_in = rest[:6]
    active = position // SPLIT == stage * planes

    @pl.when(active)
    def _():
        wide = [wide_ref.at[i] for i in range(4)]
        tight = [tight_ref.at[i] for i in range(4)]

        def keep(out):
            for c in range(2):
                for i in range(n):
                    put_plane(nat.at[c], i, n, w[c, i])
                out[c] = nat[c, :, HALO : HALO + STRIP, :]

        def one(t, out):
            heun(w, mid, w, wide, n, lambda c, i: plane(near_ref.at[t, c], i, n))
            keep(out)

        def one_tight(t, out):
            heun(w_t, mid_t, w_t, tight, n_t, lambda c, i: plane(far_ref.at[t - SPLIT, c], i, n_t))
            for c in range(2):
                for i in range(n_t):
                    put_plane(nat_t.at[c], i, n_t, w_t[c, i])
                out[c] = nat_t[c, :, INNER : INNER + STRIP, :]

        if stage == 0:
            for c in range(2):
                corr_ref[0, c] = jnp.zeros_like(corr_ref[0, c])
                for i in range(n):
                    w[c, i] = plane(near_ref.at[0, c], i, n)
            keep(corr_ref.at[1])
        else:
            even = lax.rem(position, 2) == 0
            for choice, refs_in_order in ((even, (other, own, pair)), (jnp.logical_not(even), (pair, own, other))):

                @pl.when(choice)
                def _():
                    for c in range(2):
                        for k, ref in enumerate(refs_in_order):
                            nat[c, :, k * STRIP : (k + 1) * STRIP, :] = ref[c]

            for c in range(2):
                corr_ref[0, c] = own[c]
                for i in range(n):
                    w[c, i] = plane(nat.at[c], i, n)
            one(0, corr_ref.at[1])

        def step(t, carry):
            one(t, corr_ref.at[t + 1])
            return carry

        def step_tight(t, carry):
            one_tight(t, corr_ref.at[t + 1])
            return carry

        lax.fori_loop(1, SPLIT, step, 0, unroll=True)
        for c in range(2):
            for i in range(n_t):
                w_t[c, i] = plane(nat.at[c], i, n_t, HALO - INNER)
        lax.fori_loop(SPLIT, GROUP - 1, step_tight, 0, unroll=True)
        if stage + 1 < stages:
            one_tight(GROUP - 1, last_ref)

    if stage > 0:

        @pl.when(jnp.logical_not(active))
        def _():
            corr_ref[...] = corr_in[...]


def ready_kernel(where_ref, got_ref, c_ref, clo_ref, chi_ref, n_ref, handed_ref, handed2_ref,
                 corr_ref, defect_ref, own_ref, cf_ref,
                 vnat, dbuf, sem):
    n = FINAL // 8
    rows = n_ref.shape[0]
    blocks = vnat.shape[0]
    position = where_ref[0]

    @pl.when(position == 0)
    def _():
        for c in range(2):
            dbuf[c] = jnp.zeros_like(dbuf[c])
            fill(own_ref.at[c], 0, c_ref.at[0, c], 0, rows)

    @pl.when(position != 0)
    def _():
        back = 1.0 / COARSE
        for c in range(2):
            dbuf[c] = (handed_ref[c] + handed2_ref[c]) - c_ref[0, c]
            for q in range(SPLIT):
                own_ref[c, :, q * STRIP : (q + 1) * STRIP, :] = back * got_ref[q, c]

    both = pl.ds(0, 2)
    pairs = [(dbuf, defect_ref.at[0])]
    for b in range(blocks):
        pairs.append((own_ref.at[both, b], corr_ref.at[0, both, :, cut(b)]))
    started = copies(pairs, sem)
    fill(vnat, 0, clo_ref.at[2], EDGE - HALO, HALO)
    fill(vnat, HALO, n_ref, 0, rows)
    fill(vnat, HALO + rows, chi_ref.at[2], 0, HALO)
    make_coefs(load_planes(vnat, n), coarse_size / STEPS, [cf_ref.at[i] for i in range(4)])
    for copy in started:
        copy.wait()


def final_kernel(where_ref, own_ref, lo_ref, hi_ref, clo_ref, chi_ref, cf_ref,
                 adv_ref,
                 nat, anat, w, mid, sem):
    n = FINAL // 8
    rows = own_ref.shape[2]
    blocks = nat.shape[1]
    position = where_ref[0]
    coef = [cf_ref.at[i] for i in range(4)]

    @pl.when(position == 0)
    def _():
        for c in range(2):
            fill(nat.at[c], 0, clo_ref.at[c], EDGE - HALO, HALO)
            fill(nat.at[c], HALO + rows, chi_ref.at[c], 0, HALO)

    @pl.when(position != 0)
    def _():
        back = 1.0 / COARSE
        for c in range(2):
            nat[c, :, 0:HALO, :] = back * lo_ref[c]
            nat[c, :, HALO + rows :, :] = back * hi_ref[c]

    both = pl.ds(0, 2)
    mine = pl.ds(HALO, rows)
    for c in range(2):
        nat[c, :, HALO : HALO + rows, :] = own_ref[c]
        for i in range(n):
            w[c, i] = FINE * plane(nat.at[c], i, n)

    def step(_, carry):
        heun(w, mid, w, coef, n)
        return carry

    lax.fori_loop(0, STEPS, step, 0, unroll=2)
    started = []
    for b in range(blocks):
        for c in range(2):
            for i in range(n):
                part = w[c, i, :, b * LANES : (b + 1) * LANES]
                anat[c, b, pl.ds(i, 8, stride=n), :] = part * (1.0 / FINE)
        pair = (anat.at[both, b, mine, :], adv_ref.at[0, both, :, cut(b)])
        started += copies([pair], sem.at[pl.ds(b, 1)])
    for copy in started:
        copy.wait()


VMEM = pl.BlockSpec(memory_space=pltpu.VMEM)
SMEM = pl.BlockSpec(memory_space=pltpu.SMEM)
ANY = pl.BlockSpec(memory_space=pl.ANY)
HBM = pl.BlockSpec(memory_space=pltpu.HBM)
FULL = pltpu.CompilerParams(vmem_limit_bytes=63 * 1024 * 1024)
PARAMS = pltpu.CompilerParams(vmem_limit_bytes=48 * 1024 * 1024)


def shards(c_values, viscosity):
    _, _, rows, cols = c_values.shape
    blocks = cols // LANES
    ring = lax.axis_size("space")
    intervals = lax.axis_size("tm")
    stages = intervals // GROUP
    up = [(i, (i + 1) % ring) for i in range(ring)]
    down = [(b, a) for a, b in up]
    where = lax.axis_index("tm").reshape(1).astype(jnp.int32)
    shape = lambda *s: jax.ShapeDtypeStruct(s, f32)
    vm = lambda *s: pltpu.VMEM(s, f32)
    dma = lambda k: pltpu.SemaphoreType.DMA((k,))

    top, bottom = pl.pallas_call(
        edges_kernel,
        out_shape=(shape(3, EDGE, cols),) * 2,
        in_specs=[HBM] * 2,
        out_specs=(ANY,) * 2,
        scratch_shapes=[vm(2, 3, EDGE, cols), dma(8)],
        compiler_params=FULL,
        name="edges",
    )(c_values, viscosity)
    own = pl.pallas_call(
        load_kernel,
        out_shape=shape(3, rows, cols),
        in_specs=[ANY] * 2,
        out_specs=ANY,
        scratch_shapes=[dma(2)],
        compiler_params=PARAMS,
        cost_estimate=pl.CostEstimate(flops=0, bytes_accessed=6 * rows * cols * 4, transcendentals=0),
        name="load",
    )(c_values, viscosity)
    lo = lax.ppermute(bottom, "space", up)
    hi = lax.ppermute(top, "space", down)

    n = 16
    window = shape(SPLIT, 2, blocks, WINDOW, LANES)
    inner = shape(2, blocks, TIGHT, LANES)
    forward, nwin, *sent = pl.pallas_call(
        forward_kernel,
        out_shape=(shape(2, rows, cols), shape(blocks, WINDOW, LANES)) + (window,) + (inner,) * SPLIT,
        in_specs=[SMEM, VMEM, VMEM, VMEM],
        out_specs=(HBM,) + (VMEM,) * (2 + SPLIT),
        scratch_shapes=[
            vm(3, blocks, 128, LANES), vm(2, blocks, 128, LANES),
            vm(2, n, 8, cols), vm(2, n, 8, cols), vm(2, n, 8, cols),
            vm(4, n + 1, 8, cols), vm(4, n + 1, 8, cols), dma(blocks),
        ],
        compiler_params=PARAMS,
        name="forward",
    )(where, own, lo, hi)

    n, n_t = WINDOW // 8, TIGHT // 8
    coefs = pl.pallas_call(
        prep_kernel,
        out_shape=(shape(4, n + 1, 8, cols), shape(4, n_t + 1, 8, cols)),
        in_specs=[VMEM],
        out_specs=(VMEM, VMEM),
        compiler_params=PARAMS,
        name="prep",
    )(nwin)

    planes = range(0, intervals, SPLIT)
    gathered = [sent[0]]
    four = [[p + q for q in range(SPLIT)] for p in planes]
    near = lax.all_to_all(sent[0], "tm", 0, 0, axis_index_groups=four)
    gathered = [near]
    for k in FAR_ORDER:
        pairs = []
        for p in range(0, intervals, GROUP):
            for q in range(SPLIT):
                a, b = p + SPLIT + q, p + (q + k) % SPLIT
                pairs += [(a, b), (b, a)]
        gathered.append(lax.ppermute(sent[1 + k], "tm", pairs))
    groups = [[g * GROUP + j for j in range(GROUP)] for g in range(stages)]

    strips = ring * SPLIT
    pieces, handed = [], []
    for stage in range(stages):
        carries = stage in (1, stages - 2)
        extra = ([forward] if carries else []) + (handed if stage == stages - 1 else [])
        operands = [where, *coefs] + extra + (gathered if stage == 0 else [*taus, *pieces, corr])
        specs = [SMEM, VMEM, VMEM] + [HBM] * len(extra) + [VMEM] * (len(operands) - 3 - len(extra))
        shapes = [shape(2, rows, cols) if carries else shape(8, LANES)]
        if stage == 0:
            shapes += [shape(SPLIT, 2, blocks, TIGHT, LANES)]
        shapes += [shape(GROUP, 2, blocks, STRIP, LANES)]
        shapes += [shape(2, blocks, STRIP, LANES)] if stage + 1 < stages else []
        aliases = {len(operands) - 1: 1} if stage > 0 else {}
        if carries:
            aliases[3] = 0
        done = pl.pallas_call(
            functools.partial(chain_kernel, stage, stages, len(extra)),
            out_shape=tuple(shapes),
            in_specs=specs,
            out_specs=(HBM,) + (VMEM,) * (len(shapes) - 1),
            scratch_shapes=[
                vm(2, blocks, WINDOW, LANES), vm(2, n, 8, cols), vm(2, n, 8, cols),
                vm(2, blocks, TIGHT, LANES), vm(2, n_t, 8, cols), vm(2, n_t, 8, cols),
            ],
            input_output_aliases=aliases,
            compiler_params=PARAMS,
            name="chain%d" % stage,
        )(*operands)
        if stage == 0:
            taus = [near, done[1]]
        corr, last = done[-2:] if stage + 1 < stages else (done[-1], None)
        if carries:
            forward = done[0]
            chain = [g * GROUP + q for g in range(2) for q in range(SPLIT)]
            pairs = [(i, i + 1) for i in range(intervals - 1) if (i in chain or i + 1 in chain) == (stage == stages - 2)]
            handed = handed + [lax.ppermute(forward, "tm", pairs)]
        if stage + 1 < stages:
            pieces = []
            moves = (lambda q: q, lambda q: q + 1 - 2 * (q % 2), lambda q: (q - 1 + 2 * (q % 2)) % strips)
            for move in moves:
                pairs = []
                for strip in range(strips):
                    to = move(strip)
                    source = stage * GROUP + strip % SPLIT
                    target = (stage + 1) * GROUP + to % SPLIT
                    pairs.append((source * ring + strip // SPLIT, target * ring + to // SPLIT))
                pieces.append(lax.ppermute(last, ("tm", "space"), pairs))

    got = lax.all_to_all(corr, "tm", 0, 0, axis_index_groups=groups)
    above = lax.ppermute(got[SPLIT - 1], "space", up)
    below = lax.ppermute(got[0], "space", down)

    n = FINAL // 8
    corrected, defect, mine, cf = pl.pallas_call(
        ready_kernel,
        out_shape=(shape(1, 2, rows, cols),) * 2 + (shape(2, blocks, rows, LANES), shape(4, n + 1, 8, cols)),
        in_specs=[SMEM] + [VMEM] * 7,
        out_specs=(ANY, ANY, VMEM, VMEM),
        scratch_shapes=[vm(blocks, FINAL, LANES), vm(2, rows, cols), dma(1 + blocks)],
        compiler_params=PARAMS,
        cost_estimate=pl.CostEstimate(flops=10**6, bytes_accessed=2**21, transcendentals=0),
        name="ready",
    )(where, got, c_values, lo, hi, viscosity, *handed)
    advanced = pl.pallas_call(
        final_kernel,
        out_shape=shape(1, 2, rows, cols),
        in_specs=[SMEM] + [VMEM] * 6,
        out_specs=ANY,
        scratch_shapes=[
            vm(2, blocks, FINAL, LANES), vm(2, blocks, FINAL, LANES),
            vm(2, n, 8, cols), vm(2, n, 8, cols), dma(blocks),
        ],
        compiler_params=PARAMS,
        name="final",
    )(where, mine, above, below, lo, hi, cf)
    return corrected, advanced, defect


def solution(mesh):
    return jax.shard_map(
        shards,
        mesh=mesh,
        in_specs=(P("tm", None, "space", None), P("space", None)),
        out_specs=(P("tm", None, "space", None),) * 3,
        check_vma=False,
    )
```
